32 devices in a mesh: depth: 4 (over x, core), gy: 4 (over z), gx: 2 (over y).
Axes of the slice: x: 2, y: 2, z: 4, core: 2. Of those that a mesh axis runs over, the one named last changes fastest.
Arguments:
- conserved_thermal_state: float32 [16, 2048, 512], P('depth', 'gy', 'gx'), may hold values from -2 to 30
- tier_depth_span: float32 [16], P('depth'), may hold values from 93.75 to 562.5
- water_tier_tally: int32 [2048, 512], P('gy', 'gx'), may hold values from 0 to 16
- regrid_sender_piece: int32 [4, 2, 2, 512], P('gy', 'gx'), may hold values from 0 to 1023
- regrid_receiver_piece: int32 [4, 2, 2, 512], P('gy', 'gx'), may hold values from 0 to 1023
- regrid_piece_coefficients: bfloat16 [4, 2, 2, 512, 16, 128], P('gy', 'gx'), may hold values from -0.5 to 0.5
- baseline_means: float32 [4, 512, 256], P('depth', 'gy', 'gx'), may hold values from 5 to 25
Outputs:
- anomaly: float32 [4, 512, 256], P('depth', 'gy', 'gx')
The draws below stay inside these ranges and needn't reach their ends.
All inputs are finite; a program needn't handle non-finite values.
Results may differ from the reference program's by a relative error of at most 0.0003.
Values sent between devices are 32-bit elements; how exact they have to be, the bound alone decides.
A program may use at most 64 MiB of HBM per device.

```python
import math
import jax
import jax.numpy as jnp
from jax import lax

JT = 512
IT = 256
SB = 128
TB = 16
SMOOTH = 2
VERTICAL_TIERS = 16
INPUT_GRID_SPAN = 2048
INPUT_GRID_WIDTH = 512
BLK_DEV = 1024
CAP = 512
TJ = 128
TI = 128
TBLK = 1024
NJ_T = 512
NI_T = 256
N_GY = 4
N_GX = 2


def touch_ends(result, own_key, low, top_value):
    dims = result.shape
    spot = [jax.random.randint(jax.random.fold_in(own_key, axis), (), 0, dims[axis]) for axis in range(len(dims))]
    result = result.at[tuple(spot)].set(low)
    longest = dims.index(max(dims))
    spot[longest] = (spot[longest] + 1) % dims[longest]
    return result.at[tuple(spot)].set(top_value)


def levels(key, extent, split, smallest, top_value):
    gain = 1.0
    for position, shards_of in split:
        draws = jax.random.uniform(jax.random.fold_in(jax.random.fold_in(key, 6), position), (shards_of,), jnp.float32, smallest / len(split), top_value / len(split))
        gain = gain * jnp.repeat(jnp.exp(draws), extent[position] // shards_of).reshape((-1,) + (1,) * (len(extent) - 1 - position))
    return gain


def normal_values(own_key, extent, width, limit, pieces=(), kind=jnp.bfloat16):
    values = width * jax.random.normal(own_key, extent, jnp.float32)
    if pieces:
        values = values * levels(own_key, extent, pieces, -0.22, 0.18)
    return jnp.clip(values, -limit, limit).astype(kind)


def setup_inputs(seed: int = 0) -> dict:
    keys = jax.random.split(jax.random.key(seed), 8)
    return {
        "conserved_thermal_state": jnp.clip(-2.0 + 32.0 * jax.random.uniform(keys[0], (VERTICAL_TIERS, INPUT_GRID_SPAN, INPUT_GRID_WIDTH), jnp.float32) ** levels(keys[0], (VERTICAL_TIERS, INPUT_GRID_SPAN, INPUT_GRID_WIDTH), ((0, 4), (1, 4), (2, 2)), -0.2, 0.2), -2.0, 30.0),
        "tier_depth_span": jnp.clip(jnp.exp(math.log(562.5) - 1.7917595 * jax.random.uniform(keys[1], (VERTICAL_TIERS,), jnp.float32) ** levels(keys[1], (VERTICAL_TIERS,), ((0, 4),), -0.2, 0.2)), 93.75, 562.5),
        "water_tier_tally": touch_ends(jax.random.randint(keys[2], (INPUT_GRID_SPAN, INPUT_GRID_WIDTH), 0, VERTICAL_TIERS + 1), jax.random.fold_in(keys[2], 1), 0, VERTICAL_TIERS).astype(jnp.int32),
        "regrid_sender_piece": touch_ends(jax.random.randint(keys[3], (N_GY, N_GX, N_GX, CAP), 0, BLK_DEV), jax.random.fold_in(keys[3], 1), 0, BLK_DEV - 1).astype(jnp.int32),
        "regrid_receiver_piece": touch_ends(jax.random.randint(keys[4], (N_GY, N_GX, N_GX, CAP), 0, TBLK), jax.random.fold_in(keys[4], 1), 0, TBLK - 1).astype(jnp.int32),
        "regrid_piece_coefficients": normal_values(keys[5], (N_GY, N_GX, N_GX, CAP, TB, SB), SB ** -0.5, 0.5, ((0, 4), (1, 2))),
        "baseline_means": jnp.clip(5.0 + 20.0 * jax.random.uniform(keys[6], (4, NJ_T, NI_T), jnp.float32) ** levels(keys[6], (4, NJ_T, NI_T), ((0, 4), (1, 4), (2, 2)), -0.2, 0.2), 5.0, 25.0),
    }


cp_zero = 3991.86795711963
vol_zero = 9.7e-4
therm_one = 1.7e-4
therm_two = 5.0e-6
compress = 4.4e-6
bounds = (300.0, 700.0, 2000.0)
full_norm = 4000.0
smooth_nu = 0.2


def tier_enthalpy_store(temp_layer, ocean_gauge_stress):
    expand = 1.0 + therm_one * temp_layer + therm_two * temp_layer * temp_layer
    volume = vol_zero * (expand - compress * ocean_gauge_stress)
    enthalpy = cp_zero * temp_layer + 1.0e4 * vol_zero * (expand * ocean_gauge_stress - 0.5 * compress * ocean_gauge_stress * ocean_gauge_stress)
    return enthalpy / (volume * (cp_zero / vol_zero))


def depth_weights(level_tops, tier_depth_span):
    fractions = [jnp.clip(bound_depth - level_tops, 0.0, tier_depth_span) / bound_depth for bound_depth in bounds]
    fractions.append(tier_depth_span / full_norm)
    return jnp.stack(fractions)


def pad_north_fold(surface):
    north_row = surface[-1:, ::-1]
    south_row = jnp.zeros_like(north_row)
    stacked = jnp.concatenate([south_row, surface, north_row], 0)
    return jnp.concatenate([stacked[:, -1:], stacked, stacked[:, :1]], 1)


def smooth(surface, wet_mask, wet_pad):
    padded = pad_north_fold(surface)
    net_flux = wet_pad[:-2, 1:-1] * (padded[:-2, 1:-1] - surface)
    net_flux = net_flux + wet_pad[2:, 1:-1] * (padded[2:, 1:-1] - surface)
    net_flux = net_flux + wet_pad[1:-1, :-2] * (padded[1:-1, :-2] - surface)
    net_flux = net_flux + wet_pad[1:-1, 2:] * (padded[1:-1, 2:] - surface)
    return surface + smooth_nu * wet_mask * net_flux


def reference(conserved_thermal_state, tier_depth_span, water_tier_tally, regrid_sender_piece, regrid_receiver_piece, regrid_piece_coefficients, baseline_means):
    level_tops = jnp.concatenate([jnp.zeros((1,), jnp.float32), jnp.cumsum(tier_depth_span)[:-1]])
    ocean_gauge_stress = level_tops + 0.5 * tier_depth_span
    scaling_coefficients = depth_weights(level_tops, tier_depth_span)

    def gather_tier_share(running, level_item):
        temp_layer, level_press, weight_col, level_index = level_item
        water_tier_indicator = (level_index < water_tier_tally).astype(jnp.float32)
        heat_layer = tier_enthalpy_store(temp_layer, level_press) * water_tier_indicator
        return running + weight_col[:, None, None] * heat_layer[None], None

    tier_indices = jnp.arange(VERTICAL_TIERS, dtype=jnp.int32)
    starting_tally = jnp.zeros((4, INPUT_GRID_SPAN, INPUT_GRID_WIDTH), jnp.float32)
    vertical_total_over_depth, discarded_entry = lax.scan(gather_tier_share, starting_tally, (conserved_thermal_state, ocean_gauge_stress, scaling_coefficients.T, tier_indices))

    wet_mask = (water_tier_tally > 0).astype(jnp.float32)
    wet_pad = pad_north_fold(wet_mask)

    def smooth_all(surface):
        for sweep_index in range(SMOOTH):
            surface = smooth(surface, wet_mask, wet_pad)
        return surface

    smoothed = jax.vmap(smooth_all)(vertical_total_over_depth)

    row_ids = jnp.arange(N_GY, dtype=jnp.int32)[:, None, None, None]
    col_ids = jnp.arange(N_GX, dtype=jnp.int32)[None, None, :, None]
    segment_ids = ((row_ids * N_GX + col_ids) * TBLK + regrid_receiver_piece).reshape(-1)

    def remap_one(surface):
        tile_blocks = surface.reshape(N_GY, JT, N_GX, IT).transpose(0, 2, 1, 3).reshape(N_GY, N_GX, BLK_DEV, SB)

        def row_blocks(row_item):
            tile_row, sources, weight_row = row_item
            picked = jax.vmap(lambda blocks, index_list: jnp.take(blocks, index_list, axis=0))(tile_row, sources.reshape(N_GX, N_GX * CAP))
            picked = picked.reshape(N_GX, N_GX, CAP, SB)
            return jnp.einsum('bcstq,bcsq->bcst', weight_row.astype(jnp.float32), picked, precision=lax.Precision.HIGHEST)

        contrib = lax.map(row_blocks, (tile_blocks, regrid_sender_piece, regrid_piece_coefficients))
        summed = jax.ops.segment_sum(contrib.reshape(-1, TB), segment_ids, num_segments=N_GY * N_GX * TBLK)
        summed = summed.reshape(N_GY, N_GX, TJ, TI).transpose(0, 2, 1, 3)
        return summed.reshape(NJ_T, NI_T)

    remapped = lax.map(remap_one, smoothed)
    return remapped - baseline_means
```

```python
import functools

import jax
import jax.numpy as jnp
from jax import lax
from jax.experimental import pallas as pl
from jax.experimental.pallas import tpu as pltpu
from jax.sharding import PartitionSpec as P

SB = 128
TB = 16

cp_zero = 3991.86795711963
vol_zero = 0.00097
therm_one = 0.00017
therm_two = 5e-06
compress = 4.4e-06
bounds = (300.0, 700.0, 2000.0)
full_norm = 4000.0
smooth_nu = 0.2

MESH = pl.DeviceIdType.MESH
F32 = jnp.float32
BF16 = jnp.bfloat16
PAD = 8


def lanes(shape):
    return lax.broadcasted_iota(jnp.int32, shape, len(shape) - 1)


def sublanes(shape):
    return lax.broadcasted_iota(jnp.int32, shape, len(shape) - 2)


def split_two(x):
    hi = x.astype(BF16)
    lo = (x - hi.astype(F32)).astype(BF16)
    return hi, lo


def kernel(
    nd, ny, nx, cap, unroll,
    span_s, pick_s, temp_h, tally_v, tgt_v, coef_h, base_v,
    out_v,
    temp_v, coef_v, fa, fb, acoef, store, pack, pin, pint,
    col_out, col_in, row_out, row_in, th_out, th_in, prm,
    vout, vin, tslot, onehot, eexp,
    temp_sem, coef_sem, col_ss, col_rs, row_ss, row_rs, th_ss, th_rs, tg_ss, tg_rs, v_ss, v_rs,
):
    d, y, b = lax.axis_index("depth"), lax.axis_index("gy"), lax.axis_index("gx")
    nl, rows, cols = temp_v.shape
    chunks = temp_sem.shape[0]
    crow = rows // chunks
    last = ny - 1
    east, west = lax.rem(b + 1, nx), lax.rem(b + nx - 1, nx)
    mirror = nx - 1 - b

    temp_copies = []
    for q in range(chunks):
        span = pl.ds(q * crow, crow)
        copy = pltpu.make_async_copy(temp_h.at[:, span, :], temp_v.at[:, span, :], temp_sem.at[q])
        copy.start()
        temp_copies.append(copy)
    coef_copies = []
    for j in list(range(1, nx)) + [0]:
        c = lax.rem(b + j, nx)
        copy = pltpu.make_async_copy(coef_h.at[c], coef_v.at[j], coef_sem.at[j])
        copy.start()
        coef_copies.append(copy)

    row_in[...] = jnp.zeros(row_in.shape, F32)

    barrier = pltpu.get_barrier_semaphore()
    peers = [(i, j) for i in range(nd) for j in range(nx) if (i, j) != (0, 0)]
    for i, j in peers:
        pl.semaphore_signal(
            barrier, inc=1, device_id=(lax.rem(d + i, nd), y, lax.rem(b + j, nx)), device_id_type=MESH
        )

    @pl.when(y > 0)
    def _():
        pl.semaphore_signal(barrier, inc=1, device_id=(d, y - 1, b), device_id_type=MESH)

    @pl.when(y < last)
    def _():
        pl.semaphore_signal(barrier, inc=1, device_id=(d, y + 1, b), device_id_type=MESH)

    thick = [span_s[l] for l in range(nl)]
    total = thick[0]
    for l in range(1, nl):
        total = total + thick[l]
    th_out[...] = jnp.full(th_out.shape, total, F32)
    zero_rows = jnp.zeros((PAD, cols), F32)
    for m in range(5):
        for buf in (fa, fb):
            buf[m, 0:PAD, :] = zero_rows
            buf[m, PAD + rows:, :] = zero_rows
    pint[...] = jnp.zeros(pint.shape, F32)
    col_out[...] = jnp.zeros(col_out.shape, F32)
    row_out[...] = jnp.zeros(row_out.shape, F32)

    inner = jnp.logical_and(y > 0, y < last)

    @pl.when(inner)
    def _():
        pl.semaphore_wait(barrier, len(peers) + 2)

    @pl.when(jnp.logical_not(inner))
    def _():
        pl.semaphore_wait(barrier, len(peers) + 1)

    th_copies = []
    for i in range(1, nd):
        copy = pltpu.make_async_remote_copy(
            th_out, th_in.at[i], th_ss.at[i], th_rs.at[i], (lax.rem(d + i, nd), y, b), MESH
        )
        copy.start()
        th_copies.append(copy)
    tg_copies = []
    for j in range(1, nx):
        c = lax.rem(b + j, nx)
        copy = pltpu.make_async_remote_copy(
            tgt_v.at[c], tslot.at[j], tg_ss.at[j], tg_rs.at[j], (d, y, c), MESH
        )
        copy.start()
        tg_copies.append(copy)
    tslot[0] = tgt_v[b]

    top = jnp.zeros((8, 128), F32)
    for i in range(1, nd):
        th_copies[i - 1].wait()
        top = top + jnp.where(d >= i, th_in[i], 0.0)
    alpha = 10000.0 * vol_zero / cp_zero
    for l in range(nl):
        press = top + 0.5 * thick[l]
        prm[l, 0] = alpha * press
        prm[l, 1] = (0.5 * alpha * compress) * press * press
        prm[l, 2] = compress * press
        for k, depth in enumerate(bounds):
            prm[l, 3 + k] = jnp.clip(depth - top, 0.0, thick[l]) / depth
        prm[l, 6] = jnp.full((8, 128), thick[l] / full_norm, F32)
        top = top + thick[l]

    lane = lanes((8, 128))
    first_lane, last_lane = lane == 0, lane == 127
    row_tile = lambda r: pl.multiple_of(r * 8, 8)

    def pack_edges(pairs):
        packed = jnp.zeros((8, 128), F32)
        for m, (left, right) in enumerate(pairs):
            edge = jnp.where(first_lane, left, right)
            packed = jnp.where((lane >> 1) == m, pltpu.roll(edge, 2 * m + 1, 1), packed)
        return packed

    def heat_rows(r, carry):
        base = row_tile(r)
        pairs = [[None, None] for _ in range(5)]
        for h in range(2):
            here = (pl.ds(base, 8), slice(128 * h, 128 * h + 128))
            tally = tally_v[here]
            sums = [None] * 4
            for l in range(nl):
                t = temp_v[(l,) + here]
                expand = 1.0 + t * (therm_one + therm_two * t)
                heat = (t + prm[l, 0] * expand - prm[l, 1]) / (expand - prm[l, 2])
                heat = jnp.where(d * nl + l < tally, heat, 0.0)
                for k in range(4):
                    term = prm[l, 3 + k] * heat
                    sums[k] = term if l == 0 else sums[k] + term
            sums.append(jnp.where(tally > 0, 1.0, 0.0))
            for m in range(5):
                fa[m, pl.ds(base + PAD, 8), 128 * h:128 * h + 128] = sums[m]
                pairs[m][h] = sums[m]
        pack[pl.ds(base, 8), :] = pack_edges(pairs)
        return carry

    for q in range(chunks):
        temp_copies[q].wait()
        lax.fori_loop(q * crow // 8, (q + 1) * crow // 8, heat_rows, 0, unroll=2)

    def send_edges(e, buf):
        for q in range(rows // 128):
            span = slice(128 * q, 128 * q + 128)
            turned = pack[span, :].T
            for m in range(5):
                col_out[e, 0, m:m + 1, span] = turned[2 * m:2 * m + 1]
                col_out[e, 1, m:m + 1, span] = turned[2 * m + 1:2 * m + 2]
        for m in range(5):
            src = fa if m == 4 else buf
            row_out[e, 0, m:m + 1, :] = src[m, PAD + rows - 1:PAD + rows, :]
            row_out[e, 1, m:m + 1, :] = src[m, PAD:PAD + 1, :]
        to_east = pltpu.make_async_remote_copy(
            col_out.at[e, 0], col_in.at[e, 0], col_ss.at[e, 0], col_rs.at[e, 0], (d, y, east), MESH
        )
        to_west = pltpu.make_async_remote_copy(
            col_out.at[e, 1], col_in.at[e, 1], col_ss.at[e, 1], col_rs.at[e, 1], (d, y, west), MESH
        )
        to_east.start()
        to_west.start()

        @pl.when(y < last)
        def _():
            pltpu.make_async_remote_copy(
                row_out.at[e, 0], row_in.at[e, 1], row_ss.at[e, 0], row_rs.at[e, 1], (d, y + 1, b), MESH
            ).start()

        @pl.when(y == last)
        def _():
            pltpu.make_async_remote_copy(
                row_out.at[e, 0], row_in.at[e, 0], row_ss.at[e, 0], row_rs.at[e, 0], (d, y, mirror), MESH
            ).start()

        @pl.when(y > 0)
        def _():
            pltpu.make_async_remote_copy(
                row_out.at[e, 1], row_in.at[e, 0], row_ss.at[e, 1], row_rs.at[e, 0], (d, y - 1, b), MESH
            ).start()

        return to_east, to_west

    def receive_edges(e, copies):
        for copy in copies:
            copy.wait()
        north = pltpu.make_async_remote_copy(
            row_out.at[e, 0], row_in.at[e, 0], row_ss.at[e, 0], row_rs.at[e, 0], (d, y, mirror), MESH
        )
        north.wait_send()
        north.wait_recv()

        @pl.when(y > 0)
        def _():
            south = pltpu.make_async_remote_copy(
                row_out.at[e, 1], row_in.at[e, 1], row_ss.at[e, 1], row_rs.at[e, 1], (d, y - 1, b), MESH
            )
            south.wait_send()
            south.wait_recv()

        @pl.when(y == last)
        def _():
            shape = (cols, cols)
            flip = jnp.where(lanes(shape) + sublanes(shape) == cols - 1, 1.0, 0.0)
            row_in[e, 0] = jnp.dot(
                row_in[e, 0], flip, precision=lax.Precision.HIGHEST, preferred_element_type=F32
            )

        for m in range(5):
            pint[2 * m:2 * m + 1, :] = col_in[e, 1, m:m + 1, :]
            pint[2 * m + 1:2 * m + 2, :] = col_in[e, 0, m:m + 1, :]
        for q in range(rows // 128):
            span = slice(128 * q, 128 * q + 128)
            pin[span, :] = pint[:, span].T

    tall = 32

    def neighbours(buf, m, base):
        wide = lanes((tall, cols))
        around = buf[m, pl.ds(base, tall + 2 * PAD), :]
        here = around[PAD:PAD + tall]
        up = around[PAD + 1:PAD + 1 + tall]
        down = around[PAD - 1:PAD - 1 + tall]
        left = jnp.where(wide == 0, 0.0, pltpu.roll(here, 1, 1))
        right = jnp.where(wide == cols - 1, 0.0, pltpu.roll(here, cols - 1, 1))
        return here, (up + down) + (left + right)

    def sweep(src, dst, build):
        def body(r, carry):
            base = pl.multiple_of(r * tall, tall)
            if build:
                wet, count = neighbours(fa, 4, base)
                keep = 1.0 - smooth_nu * count
                acoef[pl.ds(base, tall), :] = keep
            else:
                wet = fa[4, pl.ds(base + PAD, tall), :]
                keep = acoef[pl.ds(base, tall), :]
            gain = smooth_nu * wet
            for k in range(4):
                here, around = neighbours(src, k, base)
                dst[k, pl.ds(base + PAD, tall), :] = keep * here + gain * around
            return carry

        lax.fori_loop(0, rows // tall, body, 0)

    def fix_rows(e, src, dst):
        for side, row in ((0, PAD + rows - 1), (1, PAD)):
            wet_edge = row_in[e, side, 4:5, :]
            gain = smooth_nu * fa[4, row:row + 1, :]
            for k in range(4):
                more = gain * (row_in[e, side, k:k + 1, :] - wet_edge * src[k, row:row + 1, :])
                dst[k, row:row + 1, :] = dst[k, row:row + 1, :] + more

    def fix_columns(src, dst, base):
        here = pl.ds(base + PAD, 8)
        edges = pin[pl.ds(base, 8), :]
        wet_edge = pltpu.roll(edges, 128 - 9, 1)
        fixed = []
        for k in range(4):
            field_edge = pltpu.roll(edges, 128 - (2 * k + 1), 1)
            pair = []
            for h, mask in ((0, first_lane), (1, last_lane)):
                at = (k, here, slice(128 * h, 128 * h + 128))
                gain = smooth_nu * fa[(4,) + at[1:]]
                more = gain * (field_edge - wet_edge * src[at])
                pair.append(dst[at] + jnp.where(mask, more, 0.0))
            fixed.append(pair)
        return fixed

    edges = send_edges(0, fa)
    sweep(fa, fb, True)
    receive_edges(0, edges)
    fix_rows(0, fa, fb)

    def fix_first(r, carry):
        base = row_tile(r)
        fixed = fix_columns(fa, fb, base)
        for k in range(4):
            for h in range(2):
                fb[k, pl.ds(base + PAD, 8), 128 * h:128 * h + 128] = fixed[k][h]
        wet = [fa[4, pl.ds(base + PAD, 8), 128 * h:128 * h + 128] for h in range(2)]
        pack[pl.ds(base, 8), :] = pack_edges(fixed + [wet])
        return carry

    lax.fori_loop(0, rows // 8, fix_first, 0, unroll=2)
    edges = send_edges(1, fb)
    sweep(fb, fa, False)
    receive_edges(1, edges)
    fix_rows(1, fb, fa)

    def fix_second(r, carry):
        base = row_tile(r)
        fixed = fix_columns(fb, fa, base)
        for h in range(2):
            parts = []
            for k in range(4):
                parts.append(fixed[k][h].astype(BF16).astype(F32))
            for k in range(4):
                parts.append(fixed[k][h] - parts[k])
            block = jnp.swapaxes(jnp.stack(parts), 0, 1)
            store[pl.ds(h * rows + base, 8)] = block
        return carry

    lax.fori_loop(0, rows // 8, fix_second, 0, unroll=2)

    group = lane >> 4
    v_copies = []
    for j in list(range(1, nx)) + [0]:
        c = lax.rem(b + j, nx)
        coef_copies[(j - 1) % nx].wait()

        def remap(u, carry, c=c, j=j):
            for s in range(unroll):
                g = u * unroll + s
                picked = []
                for p in range(16):
                    at = pick_s[c * cap + g * 16 + p]
                    picked.append(store[(at & 1) * rows + (at >> 1)])
                block = jnp.concatenate(picked, axis=0).astype(BF16)
                weights = coef_v[j, pl.ds(pl.multiple_of(g * 256, 256), 256), :]
                prod = lax.dot_general(
                    block, weights, (((1,), (1,)), ((), ())), preferred_element_type=F32
                )
                for half in range(2):
                    tight = jnp.zeros((8, 128), F32)
                    for p in range(8):
                        row = (half * 8 + p) * 8
                        tight = jnp.where(
                            group == p, prod[row:row + 8, 128 * half:128 * half + 128], tight
                        )
                    tight = tight[0:4] + tight[4:8]
                    for k in range(4):
                        vout[lax.rem(k - d + nd, nd), j, pl.ds(g * 2 + half, 1), :] = tight[k:k + 1]
            return carry

        lax.fori_loop(0, cap // (16 * unroll), remap, 0)
        for i in range(nd):
            if (i, j) != (0, 0):
                copy = pltpu.make_async_remote_copy(
                    vout.at[i, j], vin.at[i, j], v_ss.at[i, j], v_rs.at[i, j],
                    (lax.rem(d + i, nd), y, c), MESH,
                )
                copy.start()
                v_copies.append(copy)

    for copy in tg_copies:
        copy.wait()
    tr = out_v.shape[0]
    for j in range(nx):
        ids = tslot[j]
        for q in range(8):
            shape = (tr, cap)
            wanted = sublanes(shape) * 8 + q
            onehot[q * tr:(q + 1) * tr, j * cap:(j + 1) * cap] = jnp.where(
                wanted == ids, 1.0, 0.0
            ).astype(BF16)
    for copy in v_copies:
        copy.wait()
    gr = cap // 8
    own_group = (lanes((gr, 8, 128)) >> 4) == lax.broadcasted_iota(jnp.int32, (gr, 8, 128), 1)
    for j in range(nx):
        summed = vout[0, 0] if j == 0 else vin[0, j]
        for i in range(1, nd):
            summed = summed + vin[i, j]
        spread = jnp.where(own_group, summed[:, None, :], 0.0).reshape(cap, 128)
        hi, lo = split_two(spread)
        eexp[j * cap:(j + 1) * cap, 0:128] = hi
        eexp[j * cap:(j + 1) * cap, 128:256] = lo
    both = jnp.dot(onehot[...], eexp[...], preferred_element_type=F32)
    hi, lo = split_two(both[:, 0:128] + both[:, 128:256])
    shape = (128, 128)
    tile16 = jnp.where((lanes(shape) & 15) == (sublanes(shape) & 15), 1.0, 0.0).astype(BF16)
    spread = jnp.dot(hi, tile16, preferred_element_type=F32) + jnp.dot(
        lo, tile16, preferred_element_type=F32
    )
    result = jnp.zeros((tr, 128), F32)
    where_q = lanes((tr, 128)) >> 4
    for q in range(8):
        result = jnp.where(where_q == q, spread[q * tr:(q + 1) * tr], result)
    out_v[...] = result - base_v[...]


def per_device(sizes, temp, span, tally, sender, receiver, coef, base):
    nd, ny, nx = sizes
    nl, rows, cols = temp.shape
    cap = sender.shape[-1]
    unroll = min(8, cap // 16)
    blocks = rows * cols // SB
    vmem = pltpu.VMEM
    dma = pltpu.SemaphoreType.DMA
    any_spec = pl.BlockSpec(memory_space=pl.ANY)
    vspec = pl.BlockSpec(memory_space=vmem)
    sspec = pl.BlockSpec(memory_space=pltpu.SMEM)
    tr, tc = base.shape[1:]
    scratch = [
        vmem((nl, rows, cols), F32),
        vmem((nx, cap * TB, SB), BF16),
        vmem((5, rows + 2 * PAD, cols), F32),
        vmem((5, rows + 2 * PAD, cols), F32),
        vmem((rows, cols), F32),
        vmem((blocks, 8, SB), F32),
        vmem((rows, 128), F32),
        vmem((rows, 128), F32),
        vmem((128, rows), F32),
        vmem((2, 2, 8, rows), F32),
        vmem((2, 2, 8, rows), F32),
        vmem((2, 2, 8, cols), F32),
        vmem((2, 2, 8, cols), F32),
        vmem((8, 128), F32),
        vmem((nd, 8, 128), F32),
        vmem((nl, 7, 8, 128), F32),
        vmem((nd, nx, cap // 8, 128), F32),
        vmem((nd, nx, cap // 8, 128), F32),
        vmem((nx, 1, cap), jnp.int32),
        vmem((8 * tr, nx * cap), BF16),
        vmem((nx * cap, 256), BF16),
        dma((4,)),
        dma((nx,)),
        dma((2, 2)), dma((2, 2)),
        dma((2, 2)), dma((2, 2)),
        dma((nd,)), dma((nd,)),
        dma((nx,)), dma((nx,)),
        dma((nd, nx)), dma((nd, nx)),
    ]
    out = pl.pallas_call(
        functools.partial(kernel, nd, ny, nx, cap, unroll),
        out_shape=jax.ShapeDtypeStruct((tr, tc), F32),
        in_specs=[sspec, sspec, any_spec, vspec, vspec, any_spec, vspec],
        out_specs=vspec,
        scratch_shapes=scratch,
        compiler_params=pltpu.CompilerParams(
            collective_id=0, has_side_effects=True, vmem_limit_bytes=48 * 1024 * 1024
        ),
    )(
        span,
        sender.reshape(-1),
        temp,
        tally,
        receiver.reshape(nx, 1, cap),
        coef.reshape(nx, cap * TB, SB),
        base[0],
    )
    return out[None]


def solution(mesh):
    sizes = tuple(mesh.shape[a] for a in ("depth", "gy", "gx"))
    return jax.shard_map(
        functools.partial(per_device, sizes),
        mesh=mesh,
        in_specs=(
            P("depth", "gy", "gx"),
            P("depth"),
            P("gy", "gx"),
            P("gy", "gx", None, None),
            P("gy", "gx", None, None),
            P("gy", "gx", None, None, None, None),
            P("depth", "gy", "gx"),
        ),
        out_specs=P("depth", "gy", "gx"),
        check_vma=False,
    )
```

```python
import functools

import jax
import jax.numpy as jnp
from jax import lax
from jax.experimental import pallas as pl
from jax.experimental.pallas import tpu as pltpu
from jax.sharding import PartitionSpec as P

SB = 128
TB = 16

cp_zero = 3991.86795711963
vol_zero = 0.00097
therm_one = 0.00017
therm_two = 5e-06
compress = 4.4e-06
bounds = (300.0, 700.0, 2000.0)
full_norm = 4000.0
smooth_nu = 0.2

MESH = pl.DeviceIdType.MESH
F32 = jnp.float32
BF16 = jnp.bfloat16
PAD = 8


def lanes(shape):
    return lax.broadcasted_iota(jnp.int32, shape, len(shape) - 1)


def sublanes(shape):
    return lax.broadcasted_iota(jnp.int32, shape, len(shape) - 2)


def split_two(x):
    hi = x.astype(BF16)
    lo = (x - hi.astype(F32)).astype(BF16)
    return hi, lo


def kernel(
    nd, ny, nx, cap, unroll,
    span_s, pick_h, temp_h, tally_h, tgt_h, coef_h, base_h,
    out_v,
    pick_s, tally_v, tgt_v, tgt_rows, base_v,
    temp_v, coef_v, fa, fb, acoef, store, pack, pin, pint,
    col_out, col_in, row_out, row_in, th_out, th_in, prm,
    vout, vin, tslot, onehot, eexp,
    in_sem, temp_sem, coef_sem, col_ss, col_rs, row_ss, row_rs, th_ss, th_rs, tg_ss, tg_rs, v_ss, v_rs,
):
    d, y, b = lax.axis_index("depth"), lax.axis_index("gy"), lax.axis_index("gx")
    nl, rows, cols = temp_v.shape
    chunks = temp_sem.shape[0]
    crow = rows // chunks
    last = ny - 1
    east, west = lax.rem(b + 1, nx), lax.rem(b + nx - 1, nx)
    mirror = nx - 1 - b

    small = []
    for n, (src, dst) in enumerate(
        ((tally_h, tally_v), (tgt_h, tgt_v), (pick_h, pick_s), (base_h, base_v))
    ):
        copy = pltpu.make_async_copy(src, dst, in_sem.at[n])
        copy.start()
        small.append(copy)
    temp_copies = []
    for q in range(chunks):
        span = pl.ds(q * crow, crow)
        copy = pltpu.make_async_copy(temp_h.at[:, span, :], temp_v.at[:, span, :], temp_sem.at[q])
        copy.start()
        temp_copies.append(copy)
    coef_copies = []
    for j in list(range(1, nx)) + [0]:
        c = lax.rem(b + j, nx)
        copy = pltpu.make_async_copy(coef_h.at[c], coef_v.at[j], coef_sem.at[j])
        copy.start()
        coef_copies.append(copy)

    row_in[...] = jnp.zeros(row_in.shape, F32)

    barrier = pltpu.get_barrier_semaphore()
    peers = [(i, j) for i in range(nd) for j in range(nx) if (i, j) != (0, 0)]
    for i, j in peers:
        pl.semaphore_signal(
            barrier, inc=1, device_id=(lax.rem(d + i, nd), y, lax.rem(b + j, nx)), device_id_type=MESH
        )

    @pl.when(y > 0)
    def _():
        pl.semaphore_signal(barrier, inc=1, device_id=(d, y - 1, b), device_id_type=MESH)

    @pl.when(y < last)
    def _():
        pl.semaphore_signal(barrier, inc=1, device_id=(d, y + 1, b), device_id_type=MESH)

    thick = [span_s[l] for l in range(nl)]
    total = thick[0]
    for l in range(1, nl):
        total = total + thick[l]
    th_out[...] = jnp.full(th_out.shape, total, F32)
    zero_rows = jnp.zeros((PAD, 128), F32)
    for m in range(5):
        for h in range(2):
            for buf in (fa, fb):
                buf[m, h, 0:PAD, :] = zero_rows
                buf[m, h, PAD + rows:, :] = zero_rows
    pint[...] = jnp.zeros(pint.shape, F32)
    col_out[...] = jnp.zeros(col_out.shape, F32)
    row_out[...] = jnp.zeros(row_out.shape, F32)

    lane = lanes((8, 128))
    tall, high = 32, 64

    def masks(count):
        wide = lanes((count, 128))
        return wide, wide == 0, wide == 127

    def wet_rows(r, carry):
        base = pl.multiple_of(r * high, high)
        for h in range(2):
            tally = tally_v[pl.ds(base, high), 128 * h:128 * h + 128]
            fa[4, h, pl.ds(base + PAD, high), :] = jnp.where(tally > 0, 1.0, 0.0)
        return carry

    def neighbours(buf, m, base):
        wide, first, final = masks(tall)
        here = [buf[m, h, pl.ds(base + PAD, tall), :] for h in range(2)]
        ahead = [pltpu.roll(x, 1, 1) for x in here]
        behind = [pltpu.roll(x, 127, 1) for x in here]
        left = [jnp.where(first, 0.0, ahead[0]), jnp.where(first, ahead[0], ahead[1])]
        right = [jnp.where(final, behind[1], behind[0]), jnp.where(final, 0.0, behind[1])]
        around = []
        for h in range(2):
            up = buf[m, h, pl.ds(base + PAD + 1, tall), :]
            down = buf[m, h, pl.ds(base + PAD - 1, tall), :]
            around.append((up + down) + (left[h] + right[h]))
        return here, around

    def count_rows(r, carry):
        base = pl.multiple_of(r * tall, tall)
        wet, count = neighbours(fa, 4, base)
        for h in range(2):
            acoef[h, pl.ds(base, tall), :] = 1.0 - smooth_nu * count[h]
        return carry

    tr = out_v.shape[0]

    def build_onehot(j):
        ids = tslot[j]
        for q in range(8):
            wanted = sublanes((tr, cap)) * 8 + q
            onehot[q * tr:(q + 1) * tr, j * cap:(j + 1) * cap] = jnp.where(
                wanted == ids, 1.0, 0.0
            ).astype(BF16)

    small[0].wait()
    lax.fori_loop(0, rows // high, wet_rows, 0)
    lax.fori_loop(0, rows // tall, count_rows, 0)
    small[1].wait()
    for j in range(nx):
        tgt_rows[j] = tgt_v[j:j + 1, :]
    tslot[0] = tgt_rows[b]

    inner = jnp.logical_and(y > 0, y < last)

    @pl.when(inner)
    def _():
        pl.semaphore_wait(barrier, len(peers) + 2)

    @pl.when(jnp.logical_not(inner))
    def _():
        pl.semaphore_wait(barrier, len(peers) + 1)

    th_copies = []
    for i in range(1, nd):
        copy = pltpu.make_async_remote_copy(
            th_out, th_in.at[i], th_ss.at[i], th_rs.at[i], (lax.rem(d + i, nd), y, b), MESH
        )
        copy.start()
        th_copies.append(copy)
    tg_copies = []
    for j in range(1, nx):
        c = lax.rem(b + j, nx)
        copy = pltpu.make_async_remote_copy(
            tgt_rows.at[c], tslot.at[j], tg_ss.at[j], tg_rs.at[j], (d, y, c), MESH
        )
        copy.start()
        tg_copies.append(copy)
    build_onehot(0)

    top = jnp.zeros((8, 128), F32)
    for i in range(1, nd):
        th_copies[i - 1].wait()
        top = top + jnp.where(d >= i, th_in[i], 0.0)
    alpha = 10000.0 * vol_zero / cp_zero
    for l in range(nl):
        press = top + 0.5 * thick[l]
        prm[l, 0] = alpha * press
        prm[l, 1] = (0.5 * alpha * compress) * press * press
        prm[l, 2] = compress * press
        for k, depth in enumerate(bounds):
            prm[l, 3 + k] = jnp.clip(depth - top, 0.0, thick[l]) / depth
        prm[l, 6] = jnp.full((8, 128), thick[l] / full_norm, F32)
        top = top + thick[l]

    def pack_edges(edges):
        wide = lanes(edges[0].shape)
        packed = jnp.zeros(edges[0].shape, F32)
        for m, edge in enumerate(edges):
            packed = jnp.where((wide >> 1) == m, pltpu.roll(edge, 2 * m + 1, 1), packed)
        return packed

    def heat_rows(r, carry):
        base = pl.multiple_of(r * tall, tall)
        first = masks(tall)[1]
        fields = []
        for h in range(2):
            here = (pl.ds(base, tall), slice(128 * h, 128 * h + 128))
            tally = tally_v[here]
            sums = [None] * 4
            for l in range(nl):
                par = [jnp.concatenate([prm[l, n]] * (tall // 8), axis=0) for n in range(7)]
                t = temp_v[(l,) + here]
                expand = 1.0 + t * (therm_one + therm_two * t)
                heat = (t + par[0] * expand - par[1]) / (expand - par[2])
                heat = jnp.where(d * nl + l < tally, heat, 0.0)
                for k in range(4):
                    term = par[3 + k] * heat
                    sums[k] = term if l == 0 else sums[k] + term
            for k in range(4):
                fa[k, h, pl.ds(base + PAD, tall), :] = sums[k]
            sums.append(fa[4, h, pl.ds(base + PAD, tall), :])
            fields.append(sums)
        pack[pl.ds(base, tall), :] = pack_edges(
            [jnp.where(first, fields[0][m], fields[1][m]) for m in range(5)]
        )
        return carry

    for q in range(chunks):
        temp_copies[q].wait()
        lax.fori_loop(q * crow // tall, (q + 1) * crow // tall, heat_rows, 0)

    def send_edges(e, buf):
        for q in range(rows // 128):
            span = slice(128 * q, 128 * q + 128)
            turned = pack[span, 0:16].T
            for m in range(5):
                col_out[e, 0, m:m + 1, span] = turned[2 * m:2 * m + 1]
                col_out[e, 1, m:m + 1, span] = turned[2 * m + 1:2 * m + 2]
        for m in range(5):
            src = fa if m == 4 else buf
            for h in range(2):
                half = slice(128 * h, 128 * h + 128)
                row_out[e, 0, m:m + 1, half] = src[m, h, PAD + rows - 1:PAD + rows, :]
                row_out[e, 1, m:m + 1, half] = src[m, h, PAD:PAD + 1, :]
        to_east = pltpu.make_async_remote_copy(
            col_out.at[e, 0], col_in.at[e, 0], col_ss.at[e, 0], col_rs.at[e, 0], (d, y, east), MESH
        )
        to_west = pltpu.make_async_remote_copy(
            col_out.at[e, 1], col_in.at[e, 1], col_ss.at[e, 1], col_rs.at[e, 1], (d, y, west), MESH
        )
        to_east.start()
        to_west.start()

        @pl.when(y < last)
        def _():
            pltpu.make_async_remote_copy(
                row_out.at[e, 0], row_in.at[e, 1], row_ss.at[e, 0], row_rs.at[e, 1], (d, y + 1, b), MESH
            ).start()

        @pl.when(y == last)
        def _():
            pltpu.make_async_remote_copy(
                row_out.at[e, 0], row_in.at[e, 0], row_ss.at[e, 0], row_rs.at[e, 0], (d, y, mirror), MESH
            ).start()

        @pl.when(y > 0)
        def _():
            pltpu.make_async_remote_copy(
                row_out.at[e, 1], row_in.at[e, 0], row_ss.at[e, 1], row_rs.at[e, 0], (d, y - 1, b), MESH
            ).start()

        return to_east, to_west

    def receive_edges(e, copies):
        for copy in copies:
            copy.wait()
        north = pltpu.make_async_remote_copy(
            row_out.at[e, 0], row_in.at[e, 0], row_ss.at[e, 0], row_rs.at[e, 0], (d, y, mirror), MESH
        )
        north.wait_send()
        north.wait_recv()

        @pl.when(y > 0)
        def _():
            south = pltpu.make_async_remote_copy(
                row_out.at[e, 1], row_in.at[e, 1], row_ss.at[e, 1], row_rs.at[e, 1], (d, y - 1, b), MESH
            )
            south.wait_send()
            south.wait_recv()

        @pl.when(y == last)
        def _():
            shape = (cols, cols)
            flip = jnp.where(lanes(shape) + sublanes(shape) == cols - 1, 1.0, 0.0)
            row_in[e, 0] = jnp.dot(
                row_in[e, 0], flip, precision=lax.Precision.HIGHEST, preferred_element_type=F32
            )

        for m in range(5):
            pint[2 * m:2 * m + 1, :] = col_in[e, 1, m:m + 1, :]
            pint[2 * m + 1:2 * m + 2, :] = col_in[e, 0, m:m + 1, :]
        for q in range(rows // 128):
            span = slice(128 * q, 128 * q + 128)
            pin[span, 0:16] = pint[:, span].T

    def sweep(src, dst):
        def body(r, carry):
            base = pl.multiple_of(r * tall, tall)
            keep = [acoef[h, pl.ds(base, tall), :] for h in range(2)]
            gain = [smooth_nu * fa[4, h, pl.ds(base + PAD, tall), :] for h in range(2)]
            for k in range(4):
                here, around = neighbours(src, k, base)
                for h in range(2):
                    dst[k, h, pl.ds(base + PAD, tall), :] = keep[h] * here[h] + gain[h] * around[h]
            return carry

        lax.fori_loop(0, rows // tall, body, 0)

    def fix_rows(e, src, dst):
        for side, row in ((0, PAD + rows - 1), (1, PAD)):
            for h in range(2):
                half = slice(128 * h, 128 * h + 128)
                wet_edge = row_in[e, side, 4:5, half]
                gain = smooth_nu * fa[4, h, row:row + 1, :]
                for k in range(4):
                    more = gain * (row_in[e, side, k:k + 1, half] - wet_edge * src[k, h, row:row + 1, :])
                    dst[k, h, row:row + 1, :] = dst[k, h, row:row + 1, :] + more

    def fix_columns(src, dst, base):
        wide, first, final = masks(high)
        here = pl.ds(base + PAD, high)
        edges = pin[pl.ds(base, high), :]
        wet_edge = pltpu.roll(edges, 128 - 9, 1)
        wet = jnp.where(first, fa[4, 0, here, :], fa[4, 1, here, :])
        gain = jnp.where(jnp.logical_or(first, final), smooth_nu * wet, 0.0)
        fixed = []
        for k in range(4):
            field_edge = pltpu.roll(edges, 128 - (2 * k + 1), 1)
            old = jnp.where(first, src[k, 0, here, :], src[k, 1, here, :])
            more = gain * (field_edge - wet_edge * old)
            fixed.append(
                [
                    dst[k, 0, here, :] + jnp.where(first, more, 0.0),
                    dst[k, 1, here, :] + jnp.where(final, more, 0.0),
                ]
            )
        return fixed, wet

    edges = send_edges(0, fa)
    sweep(fa, fb)
    receive_edges(0, edges)
    fix_rows(0, fa, fb)

    def fix_first(r, carry):
        base = pl.multiple_of(r * high, high)
        first = masks(high)[1]
        fixed, wet = fix_columns(fa, fb, base)
        for k in range(4):
            for h in range(2):
                fb[k, h, pl.ds(base + PAD, high), :] = fixed[k][h]
        pack[pl.ds(base, high), :] = pack_edges(
            [jnp.where(first, fixed[k][0], fixed[k][1]) for k in range(4)] + [wet]
        )
        return carry

    lax.fori_loop(0, rows // high, fix_first, 0)
    edges = send_edges(1, fb)
    sweep(fb, fa)
    receive_edges(1, edges)
    fix_rows(1, fb, fa)

    def fix_second(r, carry):
        base = pl.multiple_of(r * high, high)
        fixed, _ = fix_columns(fb, fa, base)
        for h in range(2):
            parts = [fixed[k][h].astype(BF16).astype(F32) for k in range(4)]
            parts += [fixed[k][h] - parts[k] for k in range(4)]
            for n in range(0, high, 8):
                block = jnp.swapaxes(jnp.stack([part[n:n + 8] for part in parts]), 0, 1)
                for m in range(8):
                    store[2 * (base + n + m) + h] = block[m]
        return carry

    lax.fori_loop(0, rows // high, fix_second, 0)
    for copy in small[2:]:
        copy.wait()

    group = lane >> 4
    v_copies = []
    for j in list(range(1, nx)) + [0]:
        c = lax.rem(b + j, nx)
        coef_copies[(j - 1) % nx].wait()

        def remap(u, carry, c=c, j=j):
            for s in range(unroll):
                g = u * unroll + s
                picked = []
                for p in range(16):
                    picked.append(store[pick_s[c, g * 16 + p]])
                block = jnp.concatenate(picked, axis=0).astype(BF16)
                weights = coef_v[j, pl.ds(pl.multiple_of(g * 256, 256), 256), :]
                prod = lax.dot_general(
                    block, weights, (((1,), (1,)), ((), ())), preferred_element_type=F32
                )
                for half in range(2):
                    tight = jnp.zeros((8, 128), F32)
                    for p in range(8):
                        row = (half * 8 + p) * 8
                        tight = jnp.where(
                            group == p, prod[row:row + 8, 128 * half:128 * half + 128], tight
                        )
                    tight = tight[0:4] + tight[4:8]
                    for k in range(4):
                        vout[lax.rem(k - d + nd, nd), j, pl.ds(g * 2 + half, 1), :] = tight[k:k + 1]
            return carry

        lax.fori_loop(0, cap // (16 * unroll), remap, 0)
        for i in range(nd):
            if (i, j) != (0, 0):
                copy = pltpu.make_async_remote_copy(
                    vout.at[i, j], vin.at[i, j], v_ss.at[i, j], v_rs.at[i, j],
                    (lax.rem(d + i, nd), y, c), MESH,
                )
                copy.start()
                v_copies.append(copy)

    for copy in tg_copies:
        copy.wait()
    for j in range(1, nx):
        build_onehot(j)
    for copy in v_copies:
        copy.wait()
    gr = cap // 8
    own_group = (lanes((gr, 8, 128)) >> 4) == lax.broadcasted_iota(jnp.int32, (gr, 8, 128), 1)
    for j in range(nx):
        summed = vout[0, 0] if j == 0 else vin[0, j]
        for i in range(1, nd):
            summed = summed + vin[i, j]
        spread = jnp.where(own_group, summed[:, None, :], 0.0).reshape(cap, 128)
        hi, lo = split_two(spread)
        eexp[j * cap:(j + 1) * cap, 0:128] = hi
        eexp[j * cap:(j + 1) * cap, 128:256] = lo
    both = jnp.dot(onehot[...], eexp[...], preferred_element_type=F32)
    hi, lo = split_two(both[:, 0:128] + both[:, 128:256])
    shape = (128, 128)
    tile16 = jnp.where((lanes(shape) & 15) == (sublanes(shape) & 15), 1.0, 0.0).astype(BF16)
    spread = jnp.dot(hi, tile16, preferred_element_type=F32) + jnp.dot(
        lo, tile16, preferred_element_type=F32
    )
    result = jnp.zeros((tr, 128), F32)
    where_q = lanes((tr, 128)) >> 4
    for q in range(8):
        result = jnp.where(where_q == q, spread[q * tr:(q + 1) * tr], result)
    out_v[...] = result - base_v[...]


def per_device(sizes, temp, span, tally, sender, receiver, coef, base):
    nd, ny, nx = sizes
    nl, rows, cols = temp.shape
    cap = sender.shape[-1]
    unroll = min(8, cap // 16)
    blocks = rows * cols // SB
    vmem = pltpu.VMEM
    dma = pltpu.SemaphoreType.DMA
    any_spec = pl.BlockSpec(memory_space=pl.ANY)
    vspec = pl.BlockSpec(memory_space=vmem)
    sspec = pl.BlockSpec(memory_space=pltpu.SMEM)
    tr, tc = base.shape[1:]
    scratch = [
        pltpu.SMEM((nx, cap), jnp.int32),
        vmem((rows, cols), jnp.int32),
        vmem((nx, cap), jnp.int32),
        vmem((nx, 1, cap), jnp.int32),
        vmem((tr, tc), F32),
        vmem((nl, rows, cols), F32),
        vmem((nx, cap * TB, SB), BF16),
        vmem((5, 2, rows + 2 * PAD, 128), F32),
        vmem((5, 2, rows + 2 * PAD, 128), F32),
        vmem((2, rows, 128), F32),
        vmem((blocks, 8, SB), F32),
        vmem((rows, 128), F32),
        vmem((rows, 128), F32),
        vmem((16, rows), F32),
        vmem((2, 2, 8, rows), F32),
        vmem((2, 2, 8, rows), F32),
        vmem((2, 2, 8, cols), F32),
        vmem((2, 2, 8, cols), F32),
        vmem((8, 128), F32),
        vmem((nd, 8, 128), F32),
        vmem((nl, 7, 8, 128), F32),
        vmem((nd, nx, cap // 8, 128), F32),
        vmem((nd, nx, cap // 8, 128), F32),
        vmem((nx, 1, cap), jnp.int32),
        vmem((8 * tr, nx * cap), BF16),
        vmem((nx * cap, 256), BF16),
        dma((4,)),
        dma((4,)),
        dma((nx,)),
        dma((2, 2)), dma((2, 2)),
        dma((2, 2)), dma((2, 2)),
        dma((nd,)), dma((nd,)),
        dma((nx,)), dma((nx,)),
        dma((nd, nx)), dma((nd, nx)),
    ]
    out = pl.pallas_call(
        functools.partial(kernel, nd, ny, nx, cap, unroll),
        out_shape=jax.ShapeDtypeStruct((tr, tc), F32),
        in_specs=[sspec] + [any_spec] * 6,
        out_specs=vspec,
        scratch_shapes=scratch,
        compiler_params=pltpu.CompilerParams(
            collective_id=0, has_side_effects=True, vmem_limit_bytes=60 * 1024 * 1024
        ),
    )(
        span,
        sender.reshape(nx, cap),
        temp,
        tally,
        receiver.reshape(nx, cap),
        coef.reshape(nx, cap * TB, SB),
        base[0],
    )
    return out[None]


def solution(mesh):
    sizes = tuple(mesh.shape[a] for a in ("depth", "gy", "gx"))
    return jax.shard_map(
        functools.partial(per_device, sizes),
        mesh=mesh,
        in_specs=(
            P("depth", "gy", "gx"),
            P("depth"),
            P("gy", "gx"),
            P("gy", "gx", None, None),
            P("gy", "gx", None, None),
            P("gy", "gx", None, None, None, None),
            P("depth", "gy", "gx"),
        ),
        out_specs=P("depth", "gy", "gx"),
        check_vma=False,
    )
```

```python
import functools

import jax
import jax.numpy as jnp
from jax import lax
from jax.experimental import pallas as pl
from jax.experimental.pallas import tpu as pltpu
from jax.sharding import PartitionSpec as P

SB = 128
TB = 16

cp_zero = 3991.86795711963
vol_zero = 0.00097
therm_one = 0.00017
therm_two = 5e-06
compress = 4.4e-06
bounds = (300.0, 700.0, 2000.0)
full_norm = 4000.0
smooth_nu = 0.2

MESH = pl.DeviceIdType.MESH
F32 = jnp.float32
BF16 = jnp.bfloat16
PAD = 8
PITCH = 9


def lanes(shape):
    return lax.broadcasted_iota(jnp.int32, shape, len(shape) - 1)


def sublanes(shape):
    return lax.broadcasted_iota(jnp.int32, shape, len(shape) - 2)


def split_two(x):
    hi = x.astype(BF16)
    lo = (x - hi.astype(F32)).astype(BF16)
    return hi, lo


def kernel(
    nd, ny, nx, cap, unroll,
    span_s, pick_h, temp_h, tally_h, tgt_h, coef_h, base_h,
    out_v,
    pick_v, pick_s, tally_v, tgt_v, tgt_rows, base_v,
    temp_v, coef_v, fa, fb, acoef, store, pack, pin, pint,
    col_out, col_in, row_out, row_in, th_out, th_in, prm,
    vout, vin, tslot, onehot, eexp,
    in_sem, temp_sem, coef_sem, col_ss, col_rs, row_ss, row_rs, th_ss, th_rs, tg_ss, tg_rs, v_ss, v_rs,
):
    d, y, b = lax.axis_index("depth"), lax.axis_index("gy"), lax.axis_index("gx")
    nl, rows, cols = temp_v.shape
    chunks = temp_sem.shape[0]
    crow = rows // chunks
    last = ny - 1
    east, west = lax.rem(b + 1, nx), lax.rem(b + nx - 1, nx)
    mirror = nx - 1 - b

    small = []
    for n, (src, dst) in enumerate(
        ((tally_h, tally_v), (tgt_h, tgt_v), (pick_h, pick_v), (base_h, base_v))
    ):
        copy = pltpu.make_async_copy(src, dst, in_sem.at[n])
        copy.start()
        small.append(copy)
    temp_copies = []
    for q in range(chunks):
        span = pl.ds(q * crow, crow)
        copy = pltpu.make_async_copy(temp_h.at[:, span, :], temp_v.at[:, span, :], temp_sem.at[q])
        copy.start()
        temp_copies.append(copy)
    coef_copies = []
    for j in list(range(1, nx)) + [0]:
        c = lax.rem(b + j, nx)
        copy = pltpu.make_async_copy(coef_h.at[c], coef_v.at[j], coef_sem.at[j])
        copy.start()
        coef_copies.append(copy)

    row_in[...] = jnp.zeros(row_in.shape, F32)

    barrier = pltpu.get_barrier_semaphore()
    peers = [(i, j) for i in range(nd) for j in range(nx) if (i, j) != (0, 0)]
    for i, j in peers:
        pl.semaphore_signal(
            barrier, inc=1, device_id=(lax.rem(d + i, nd), y, lax.rem(b + j, nx)), device_id_type=MESH
        )

    @pl.when(y > 0)
    def _():
        pl.semaphore_signal(barrier, inc=1, device_id=(d, y - 1, b), device_id_type=MESH)

    @pl.when(y < last)
    def _():
        pl.semaphore_signal(barrier, inc=1, device_id=(d, y + 1, b), device_id_type=MESH)

    thick = [span_s[l] for l in range(nl)]
    total = thick[0]
    for l in range(1, nl):
        total = total + thick[l]
    th_out[...] = jnp.full(th_out.shape, total, F32)
    zero_rows = jnp.zeros((PAD, 128), F32)
    for m in range(5):
        for h in range(2):
            for buf in (fa, fb):
                buf[m, h, 0:PAD, :] = zero_rows
                buf[m, h, PAD + rows:, :] = zero_rows
    pint[...] = jnp.zeros(pint.shape, F32)
    col_out[...] = jnp.zeros(col_out.shape, F32)
    row_out[...] = jnp.zeros(row_out.shape, F32)

    lane = lanes((8, 128))
    tall, high = 64, 128

    def masks(count):
        wide = lanes((count, 128))
        return wide, wide == 0, wide == 127

    def wet_rows(r, carry):
        base = pl.multiple_of(r * high, high)
        for h in range(2):
            tally = tally_v[pl.ds(base, high), 128 * h:128 * h + 128]
            fa[4, h, pl.ds(base + PAD, high), :] = jnp.where(tally > 0, 1.0, 0.0)
        return carry

    def neighbours(buf, m, base):
        wide, first, final = masks(tall)
        here = [buf[m, h, pl.ds(base + PAD, tall), :] for h in range(2)]
        ahead = [pltpu.roll(x, 1, 1) for x in here]
        behind = [pltpu.roll(x, 127, 1) for x in here]
        left = [jnp.where(first, 0.0, ahead[0]), jnp.where(first, ahead[0], ahead[1])]
        right = [jnp.where(final, behind[1], behind[0]), jnp.where(final, 0.0, behind[1])]
        around = []
        for h in range(2):
            up = buf[m, h, pl.ds(base + PAD + 1, tall), :]
            down = buf[m, h, pl.ds(base + PAD - 1, tall), :]
            around.append((up + down) + (left[h] + right[h]))
        return here, around

    def count_rows(r, carry):
        base = pl.multiple_of(r * tall, tall)
        wet, count = neighbours(fa, 4, base)
        for h in range(2):
            acoef[h, pl.ds(base, tall), :] = 1.0 - smooth_nu * count[h]
        return carry

    tr = out_v.shape[0]

    def build_onehot(j):
        ids = tslot[j]
        for q in range(8):
            wanted = sublanes((tr, cap)) * 8 + q
            onehot[q * tr:(q + 1) * tr, j * cap:(j + 1) * cap] = jnp.where(
                wanted == ids, 1.0, 0.0
            ).astype(BF16)

    small[0].wait()
    lax.fori_loop(0, rows // high, wet_rows, 0)
    small[2].wait()
    pick_v[...] = (pick_v[...] & 1) * (rows * PITCH) + (pick_v[...] >> 1) * PITCH
    offsets = pltpu.make_async_copy(pick_v, pick_s, in_sem.at[4])
    offsets.start()
    small[1].wait()
    for j in range(nx):
        tgt_rows[j] = tgt_v[j:j + 1, :]
    tslot[0] = tgt_rows[b]

    inner = jnp.logical_and(y > 0, y < last)

    @pl.when(inner)
    def _():
        pl.semaphore_wait(barrier, len(peers) + 2)

    @pl.when(jnp.logical_not(inner))
    def _():
        pl.semaphore_wait(barrier, len(peers) + 1)

    th_copies = []
    for i in range(1, nd):
        copy = pltpu.make_async_remote_copy(
            th_out, th_in.at[i], th_ss.at[i], th_rs.at[i], (lax.rem(d + i, nd), y, b), MESH
        )
        copy.start()
        th_copies.append(copy)
    tg_copies = []
    for j in range(1, nx):
        c = lax.rem(b + j, nx)
        copy = pltpu.make_async_remote_copy(
            tgt_rows.at[c], tslot.at[j], tg_ss.at[j], tg_rs.at[j], (d, y, c), MESH
        )
        copy.start()
        tg_copies.append(copy)
    lax.fori_loop(0, rows // tall, count_rows, 0)
    build_onehot(0)

    top = jnp.zeros((8, 128), F32)
    for i in range(1, nd):
        th_copies[i - 1].wait()
        top = top + jnp.where(d >= i, th_in[i], 0.0)
    alpha = 10000.0 * vol_zero / cp_zero
    for l in range(nl):
        press = top + 0.5 * thick[l]
        prm[l, 0] = alpha * press
        prm[l, 1] = (0.5 * alpha * compress) * press * press
        prm[l, 2] = compress * press
        for k, depth in enumerate(bounds):
            prm[l, 3 + k] = jnp.clip(depth - top, 0.0, thick[l]) / depth
        prm[l, 6] = jnp.full((8, 128), thick[l] / full_norm, F32)
        top = top + thick[l]

    def pack_edges(edges):
        wide = lanes(edges[0].shape)
        packed = jnp.zeros(edges[0].shape, F32)
        for m, edge in enumerate(edges):
            packed = jnp.where((wide >> 1) == m, pltpu.roll(edge, 2 * m + 1, 1), packed)
        return packed

    def heat_rows(r, carry):
        base = pl.multiple_of(r * tall, tall)
        first = masks(tall)[1]
        fields = []
        for h in range(2):
            here = (pl.ds(base, tall), slice(128 * h, 128 * h + 128))
            tally = tally_v[here]
            sums = [None] * 4
            for l in range(nl):
                par = [jnp.concatenate([prm[l, n]] * (tall // 8), axis=0) for n in range(7)]
                t = temp_v[(l,) + here]
                expand = 1.0 + t * (therm_one + therm_two * t)
                heat = (t + par[0] * expand - par[1]) / (expand - par[2])
                heat = jnp.where(d * nl + l < tally, heat, 0.0)
                for k in range(4):
                    term = par[3 + k] * heat
                    sums[k] = term if l == 0 else sums[k] + term
            for k in range(4):
                fa[k, h, pl.ds(base + PAD, tall), :] = sums[k]
            sums.append(fa[4, h, pl.ds(base + PAD, tall), :])
            fields.append(sums)
        pack[pl.ds(base, tall), :] = pack_edges(
            [jnp.where(first, fields[0][m], fields[1][m]) for m in range(5)]
        )
        return carry

    for q in range(chunks):
        temp_copies[q].wait()
        lax.fori_loop(q * crow // tall, (q + 1) * crow // tall, heat_rows, 0)

    def send_edges(e, buf):
        for q in range(rows // 128):
            span = slice(128 * q, 128 * q + 128)
            turned = pack[span, 0:16].T
            for m in range(5):
                col_out[e, 0, m:m + 1, span] = turned[2 * m:2 * m + 1]
                col_out[e, 1, m:m + 1, span] = turned[2 * m + 1:2 * m + 2]
        for m in range(5):
            src = fa if m == 4 else buf
            for h in range(2):
                half = slice(128 * h, 128 * h + 128)
                row_out[e, 0, m:m + 1, half] = src[m, h, PAD + rows - 1:PAD + rows, :]
                row_out[e, 1, m:m + 1, half] = src[m, h, PAD:PAD + 1, :]
        to_east = pltpu.make_async_remote_copy(
            col_out.at[e, 0], col_in.at[e, 0], col_ss.at[e, 0], col_rs.at[e, 0], (d, y, east), MESH
        )
        to_west = pltpu.make_async_remote_copy(
            col_out.at[e, 1], col_in.at[e, 1], col_ss.at[e, 1], col_rs.at[e, 1], (d, y, west), MESH
        )
        to_east.start()
        to_west.start()

        @pl.when(y < last)
        def _():
            pltpu.make_async_remote_copy(
                row_out.at[e, 0], row_in.at[e, 1], row_ss.at[e, 0], row_rs.at[e, 1], (d, y + 1, b), MESH
            ).start()

        @pl.when(y == last)
        def _():
            pltpu.make_async_remote_copy(
                row_out.at[e, 0], row_in.at[e, 0], row_ss.at[e, 0], row_rs.at[e, 0], (d, y, mirror), MESH
            ).start()

        @pl.when(y > 0)
        def _():
            pltpu.make_async_remote_copy(
                row_out.at[e, 1], row_in.at[e, 0], row_ss.at[e, 1], row_rs.at[e, 0], (d, y - 1, b), MESH
            ).start()

        return to_east, to_west

    def receive_edges(e, copies):
        for copy in copies:
            copy.wait()
        north = pltpu.make_async_remote_copy(
            row_out.at[e, 0], row_in.at[e, 0], row_ss.at[e, 0], row_rs.at[e, 0], (d, y, mirror), MESH
        )
        north.wait_send()
        north.wait_recv()

        @pl.when(y > 0)
        def _():
            south = pltpu.make_async_remote_copy(
                row_out.at[e, 1], row_in.at[e, 1], row_ss.at[e, 1], row_rs.at[e, 1], (d, y - 1, b), MESH
            )
            south.wait_send()
            south.wait_recv()

        @pl.when(y == last)
        def _():
            shape = (cols, cols)
            flip = jnp.where(lanes(shape) + sublanes(shape) == cols - 1, 1.0, 0.0)
            row_in[e, 0] = jnp.dot(
                row_in[e, 0], flip, precision=lax.Precision.HIGHEST, preferred_element_type=F32
            )

        for m in range(5):
            pint[2 * m:2 * m + 1, :] = col_in[e, 1, m:m + 1, :]
            pint[2 * m + 1:2 * m + 2, :] = col_in[e, 0, m:m + 1, :]
        for q in range(rows // 128):
            span = slice(128 * q, 128 * q + 128)
            pin[span, 0:16] = pint[:, span].T

    def sweep(src, dst):
        def body(r, carry):
            base = pl.multiple_of(r * tall, tall)
            keep = [acoef[h, pl.ds(base, tall), :] for h in range(2)]
            gain = [smooth_nu * fa[4, h, pl.ds(base + PAD, tall), :] for h in range(2)]
            for k in range(4):
                here, around = neighbours(src, k, base)
                for h in range(2):
                    dst[k, h, pl.ds(base + PAD, tall), :] = keep[h] * here[h] + gain[h] * around[h]
            return carry

        lax.fori_loop(0, rows // tall, body, 0)

    def fix_rows(e, src, dst):
        for side, row in ((0, PAD + rows - 1), (1, PAD)):
            for h in range(2):
                half = slice(128 * h, 128 * h + 128)
                wet_edge = row_in[e, side, 4:5, half]
                gain = smooth_nu * fa[4, h, row:row + 1, :]
                for k in range(4):
                    more = gain * (row_in[e, side, k:k + 1, half] - wet_edge * src[k, h, row:row + 1, :])
                    dst[k, h, row:row + 1, :] = dst[k, h, row:row + 1, :] + more

    def fix_columns(src, dst, base):
        wide, first, final = masks(high)
        here = pl.ds(base + PAD, high)
        edges = pin[pl.ds(base, high), :]
        wet_edge = pltpu.roll(edges, 128 - 9, 1)
        wet = jnp.where(first, fa[4, 0, here, :], fa[4, 1, here, :])
        gain = jnp.where(jnp.logical_or(first, final), smooth_nu * wet, 0.0)
        fixed = []
        for k in range(4):
            field_edge = pltpu.roll(edges, 128 - (2 * k + 1), 1)
            old = jnp.where(first, src[k, 0, here, :], src[k, 1, here, :])
            more = gain * (field_edge - wet_edge * old)
            fixed.append(
                [
                    dst[k, 0, here, :] + jnp.where(first, more, 0.0),
                    dst[k, 1, here, :] + jnp.where(final, more, 0.0),
                ]
            )
        return fixed, wet

    edges = send_edges(0, fa)
    sweep(fa, fb)
    receive_edges(0, edges)
    fix_rows(0, fa, fb)

    def fix_first(r, carry):
        base = pl.multiple_of(r * high, high)
        first = masks(high)[1]
        fixed, wet = fix_columns(fa, fb, base)
        for k in range(4):
            for h in range(2):
                fb[k, h, pl.ds(base + PAD, high), :] = fixed[k][h]
        pack[pl.ds(base, high), :] = pack_edges(
            [jnp.where(first, fixed[k][0], fixed[k][1]) for k in range(4)] + [wet]
        )
        return carry

    lax.fori_loop(0, rows // high, fix_first, 0)
    edges = send_edges(1, fb)
    sweep(fb, fa)
    receive_edges(1, edges)
    fix_rows(1, fb, fa)

    def fix_second(r, carry):
        base = pl.multiple_of(r * high, high)
        fixed, _ = fix_columns(fb, fa, base)
        for h in range(2):
            parts = [fixed[k][h].astype(BF16).astype(F32) for k in range(4)]
            parts += [fixed[k][h] - parts[k] for k in range(4)]
            for n in range(0, high, 8):
                start = (h * rows + n) * PITCH + base * PITCH
                for m in range(8):
                    store[pl.ds(start + m, 8, stride=PITCH), :] = parts[m][n:n + 8]
        return carry

    lax.fori_loop(0, rows // high, fix_second, 0)
    small[3].wait()
    offsets.wait()

    group = lane >> 4
    v_copies = []
    for j in list(range(1, nx)) + [0]:
        c = lax.rem(b + j, nx)
        coef_copies[(j - 1) % nx].wait()

        def remap(u, carry, c=c, j=j):
            for s in range(unroll):
                g = u * unroll + s
                picked = []
                for p in range(16):
                    picked.append(store[pl.ds(pick_s[c, g * 16 + p], 8), :])
                block = jnp.concatenate(picked, axis=0).astype(BF16)
                weights = coef_v[j, pl.ds(pl.multiple_of(g * 256, 256), 256), :]
                prod = lax.dot_general(
                    block, weights, (((1,), (1,)), ((), ())), preferred_element_type=F32
                )
                for half in range(2):
                    tight = jnp.zeros((8, 128), F32)
                    for p in range(8):
                        row = (half * 8 + p) * 8
                        tight = jnp.where(
                            group == p, prod[row:row + 8, 128 * half:128 * half + 128], tight
                        )
                    tight = tight[0:4] + tight[4:8]
                    for k in range(4):
                        vout[lax.rem(k - d + nd, nd), j, pl.ds(g * 2 + half, 1), :] = tight[k:k + 1]
            return carry

        lax.fori_loop(0, cap // (16 * unroll), remap, 0)
        copies = []
        for i in range(nd):
            if (i, j) != (0, 0):
                copy = pltpu.make_async_remote_copy(
                    vout.at[i, j], vin.at[i, j], v_ss.at[i, j], v_rs.at[i, j],
                    (lax.rem(d + i, nd), y, c), MESH,
                )
                copy.start()
                copies.append(copy)
        v_copies.append((j, copies))

    for copy in tg_copies:
        copy.wait()
    for j in range(1, nx):
        build_onehot(j)
    gr = cap // 8
    own_group = (lanes((gr, 8, 128)) >> 4) == lax.broadcasted_iota(jnp.int32, (gr, 8, 128), 1)
    both = None
    for j, copies in v_copies:
        for copy in copies:
            copy.wait()
        summed = vout[0, 0] if j == 0 else vin[0, j]
        for i in range(1, nd):
            summed = summed + vin[i, j]
        spread = jnp.where(own_group, summed[:, None, :], 0.0).reshape(cap, 128)
        hi, lo = split_two(spread)
        eexp[j * cap:(j + 1) * cap, 0:128] = hi
        eexp[j * cap:(j + 1) * cap, 128:256] = lo
        span = slice(j * cap, (j + 1) * cap)
        part = jnp.dot(onehot[:, span], eexp[span, :], preferred_element_type=F32)
        both = part if both is None else both + part
    hi, lo = split_two(both[:, 0:128] + both[:, 128:256])
    shape = (128, 128)
    tile16 = jnp.where((lanes(shape) & 15) == (sublanes(shape) & 15), 1.0, 0.0).astype(BF16)
    spread = jnp.dot(hi, tile16, preferred_element_type=F32) + jnp.dot(
        lo, tile16, preferred_element_type=F32
    )
    result = jnp.zeros((tr, 128), F32)
    where_q = lanes((tr, 128)) >> 4
    for q in range(8):
        result = jnp.where(where_q == q, spread[q * tr:(q + 1) * tr], result)
    out_v[...] = result - base_v[...]


def per_device(sizes, temp, span, tally, sender, receiver, coef, base):
    nd, ny, nx = sizes
    nl, rows, cols = temp.shape
    cap = sender.shape[-1]
    unroll = min(16, cap // 16)
    blocks = rows * cols // SB
    vmem = pltpu.VMEM
    dma = pltpu.SemaphoreType.DMA
    any_spec = pl.BlockSpec(memory_space=pl.ANY)
    vspec = pl.BlockSpec(memory_space=vmem)
    sspec = pl.BlockSpec(memory_space=pltpu.SMEM)
    tr, tc = base.shape[1:]
    scratch = [
        vmem((nx, cap), jnp.int32),
        pltpu.SMEM((nx, cap), jnp.int32),
        vmem((rows, cols), jnp.int32),
        vmem((nx, cap), jnp.int32),
        vmem((nx, 1, cap), jnp.int32),
        vmem((tr, tc), F32),
        vmem((nl, rows, cols), F32),
        vmem((nx, cap * TB, SB), BF16),
        vmem((5, 2, rows + 2 * PAD, 128), F32),
        vmem((5, 2, rows + 2 * PAD, 128), F32),
        vmem((2, rows, 128), F32),
        vmem((blocks * PITCH, SB), F32),
        vmem((rows, 128), F32),
        vmem((rows, 128), F32),
        vmem((16, rows), F32),
        vmem((2, 2, 8, rows), F32),
        vmem((2, 2, 8, rows), F32),
        vmem((2, 2, 8, cols), F32),
        vmem((2, 2, 8, cols), F32),
        vmem((8, 128), F32),
        vmem((nd, 8, 128), F32),
        vmem((nl, 7, 8, 128), F32),
        vmem((nd, nx, cap // 8, 128), F32),
        vmem((nd, nx, cap // 8, 128), F32),
        vmem((nx, 1, cap), jnp.int32),
        vmem((8 * tr, nx * cap), BF16),
        vmem((nx * cap, 256), BF16),
        dma((5,)),
        dma((4,)),
        dma((nx,)),
        dma((2, 2)), dma((2, 2)),
        dma((2, 2)), dma((2, 2)),
        dma((nd,)), dma((nd,)),
        dma((nx,)), dma((nx,)),
        dma((nd, nx)), dma((nd, nx)),
    ]
    out = pl.pallas_call(
        functools.partial(kernel, nd, ny, nx, cap, unroll),
        out_shape=jax.ShapeDtypeStruct((tr, tc), F32),
        in_specs=[sspec] + [any_spec] * 6,
        out_specs=vspec,
        scratch_shapes=scratch,
        compiler_params=pltpu.CompilerParams(
            collective_id=0, has_side_effects=True, vmem_limit_bytes=60 * 1024 * 1024
        ),
    )(
        span,
        sender.reshape(nx, cap),
        temp,
        tally,
        receiver.reshape(nx, cap),
        coef.reshape(nx, cap * TB, SB),
        base[0],
    )
    return out[None]


def solution(mesh):
    sizes = tuple(mesh.shape[a] for a in ("depth", "gy", "gx"))
    return jax.shard_map(
        functools.partial(per_device, sizes),
        mesh=mesh,
        in_specs=(
            P("depth", "gy", "gx"),
            P("depth"),
            P("gy", "gx"),
            P("gy", "gx", None, None),
            P("gy", "gx", None, None),
            P("gy", "gx", None, None, None, None),
            P("depth", "gy", "gx"),
        ),
        out_specs=P("depth", "gy", "gx"),
        check_vma=False,
    )
```

```python
import functools

import jax
import jax.numpy as jnp
from jax import lax
from jax.experimental import pallas as pl
from jax.experimental.pallas import tpu as pltpu
from jax.sharding import PartitionSpec as P

SB = 128
TB = 16

cp_zero = 3991.86795711963
vol_zero = 0.00097
therm_one = 0.00017
therm_two = 5e-06
compress = 4.4e-06
bounds = (300.0, 700.0, 2000.0)
full_norm = 4000.0
smooth_nu = 0.2

MESH = pl.DeviceIdType.MESH
F32 = jnp.float32
BF16 = jnp.bfloat16
PAD = 8
PITCH = 9


def lanes(shape):
    return lax.broadcasted_iota(jnp.int32, shape, len(shape) - 1)


def sublanes(shape):
    return lax.broadcasted_iota(jnp.int32, shape, len(shape) - 2)


def split_two(x):
    hi = x.astype(BF16)
    lo = (x - hi.astype(F32)).astype(BF16)
    return hi, lo


def kernel(
    nd, ny, nx, cap, unroll, parts,
    span_h, pick_h, temp_h, tally_h, tgt_h, coef_h, base_h,
    out_v,
    span_s, pick_v, pick_s, tally_v, tgt_v, tgt_rows, base_v,
    temp_v, coef_v, fa, fb, acoef, store, pack, pin, pint,
    col_out, col_in, row_out, row_in, th_out, th_in, prm,
    vout, vin, tslot, onehot, eexp,
    in_sem, temp_sem, coef_sem, col_ss, col_rs, row_ss, row_rs, th_ss, th_rs, tg_ss, tg_rs, v_ss, v_rs,
):
    d, y, b = lax.axis_index("depth"), lax.axis_index("gy"), lax.axis_index("gx")
    nl, rows, cols = temp_v.shape
    chunks = temp_sem.shape[0]
    crow = rows // chunks
    last = ny - 1
    east, west = lax.rem(b + 1, nx), lax.rem(b + nx - 1, nx)
    mirror = nx - 1 - b

    small = []
    for n, (src, dst) in enumerate(
        ((tally_h, tally_v), (tgt_h, tgt_v), (pick_h, pick_v), (base_h, base_v), (span_h, span_s))
    ):
        copy = pltpu.make_async_copy(src, dst, in_sem.at[n])
        copy.start()
        small.append(copy)
    temp_copies = []
    for q in range(chunks):
        span = pl.ds(q * crow, crow)
        copy = pltpu.make_async_copy(temp_h.at[:, span, :], temp_v.at[:, span, :], temp_sem.at[q])
        copy.start()
        temp_copies.append(copy)
    coef_copies = []
    for j in list(range(1, nx)) + [0]:
        c = lax.rem(b + j, nx)
        copy = pltpu.make_async_copy(coef_h.at[c], coef_v.at[j], coef_sem.at[j])
        copy.start()
        coef_copies.append(copy)

    row_in[...] = jnp.zeros(row_in.shape, F32)

    barrier = pltpu.get_barrier_semaphore()
    peers = [(i, j) for i in range(nd) for j in range(nx) if (i, j) != (0, 0)]
    for i, j in peers:
        pl.semaphore_signal(
            barrier, inc=1, device_id=(lax.rem(d + i, nd), y, lax.rem(b + j, nx)), device_id_type=MESH
        )

    @pl.when(y > 0)
    def _():
        pl.semaphore_signal(barrier, inc=1, device_id=(d, y - 1, b), device_id_type=MESH)

    @pl.when(y < last)
    def _():
        pl.semaphore_signal(barrier, inc=1, device_id=(d, y + 1, b), device_id_type=MESH)

    small[4].wait()
    thick = [span_s[l] for l in range(nl)]
    total = thick[0]
    for l in range(1, nl):
        total = total + thick[l]
    th_out[...] = jnp.full(th_out.shape, total, F32)
    zero_rows = jnp.zeros((PAD, 128), F32)
    for m in range(5):
        for h in range(2):
            for buf in (fa, fb):
                buf[m, h, 0:PAD, :] = zero_rows
                buf[m, h, PAD + rows:, :] = zero_rows
    pint[...] = jnp.zeros(pint.shape, F32)
    col_out[...] = jnp.zeros(col_out.shape, F32)
    row_out[...] = jnp.zeros(row_out.shape, F32)

    lane = lanes((8, 128))
    tall, high = 64, 128

    def masks(count):
        wide = lanes((count, 128))
        return wide, wide == 0, wide == 127

    def wet_rows(r, carry):
        base = pl.multiple_of(r * high, high)
        for h in range(2):
            tally = tally_v[pl.ds(base, high), 128 * h:128 * h + 128]
            fa[4, h, pl.ds(base + PAD, high), :] = jnp.where(tally > 0, 1.0, 0.0)
        return carry

    def neighbours(buf, m, base):
        wide, first, final = masks(tall)
        here = [buf[m, h, pl.ds(base + PAD, tall), :] for h in range(2)]
        ahead = [pltpu.roll(x, 1, 1) for x in here]
        behind = [pltpu.roll(x, 127, 1) for x in here]
        left = [jnp.where(first, 0.0, ahead[0]), jnp.where(first, ahead[0], ahead[1])]
        right = [jnp.where(final, behind[1], behind[0]), jnp.where(final, 0.0, behind[1])]
        around = []
        for h in range(2):
            up = buf[m, h, pl.ds(base + PAD + 1, tall), :]
            down = buf[m, h, pl.ds(base + PAD - 1, tall), :]
            around.append((up + down) + (left[h] + right[h]))
        return here, around

    def count_rows(r, carry):
        base = pl.multiple_of(r * tall, tall)
        wet, count = neighbours(fa, 4, base)
        for h in range(2):
            acoef[h, pl.ds(base, tall), :] = 1.0 - smooth_nu * count[h]
        return carry

    tr = out_v.shape[0]

    def build_onehot(j):
        ids = tslot[j]
        for q in range(8):
            wanted = sublanes((tr, cap)) * 8 + q
            onehot[q * tr:(q + 1) * tr, j * cap:(j + 1) * cap] = jnp.where(
                wanted == ids, 1.0, 0.0
            ).astype(BF16)

    small[0].wait()
    lax.fori_loop(0, rows // high, wet_rows, 0)
    small[2].wait()
    pick_v[...] = (pick_v[...] & 1) * (rows * PITCH) + (pick_v[...] >> 1) * PITCH
    offsets = pltpu.make_async_copy(pick_v, pick_s, in_sem.at[5])
    offsets.start()
    small[1].wait()
    for j in range(nx):
        tgt_rows[j] = tgt_v[j:j + 1, :]
    tslot[0] = tgt_rows[b]

    inner = jnp.logical_and(y > 0, y < last)

    @pl.when(inner)
    def _():
        pl.semaphore_wait(barrier, len(peers) + 2)

    @pl.when(jnp.logical_not(inner))
    def _():
        pl.semaphore_wait(barrier, len(peers) + 1)

    th_copies = []
    for i in range(1, nd):
        copy = pltpu.make_async_remote_copy(
            th_out, th_in.at[i], th_ss.at[i], th_rs.at[i], (lax.rem(d + i, nd), y, b), MESH
        )
        copy.start()
        th_copies.append(copy)
    tg_copies = []
    for j in range(1, nx):
        c = lax.rem(b + j, nx)
        copy = pltpu.make_async_remote_copy(
            tgt_rows.at[c], tslot.at[j], tg_ss.at[j], tg_rs.at[j], (d, y, c), MESH
        )
        copy.start()
        tg_copies.append(copy)
    lax.fori_loop(0, rows // tall, count_rows, 0)
    build_onehot(0)

    top = jnp.zeros((8, 128), F32)
    for i in range(1, nd):
        th_copies[i - 1].wait()
        top = top + jnp.where(d >= i, th_in[i], 0.0)
    alpha = 10000.0 * vol_zero / cp_zero
    for l in range(nl):
        press = top + 0.5 * thick[l]
        prm[l, 0] = alpha * press
        prm[l, 1] = (0.5 * alpha * compress) * press * press
        prm[l, 2] = 1.0 - compress * press
        for k, depth in enumerate(bounds):
            prm[l, 3 + k] = jnp.clip(depth - top, 0.0, thick[l]) / depth
        prm[l, 6] = jnp.full((8, 128), thick[l] / full_norm, F32)
        top = top + thick[l]

    def pack_edges(edges):
        wide = lanes(edges[0].shape)
        packed = jnp.zeros(edges[0].shape, F32)
        for m, edge in enumerate(edges):
            packed = jnp.where((wide >> 1) == m, pltpu.roll(edge, 2 * m + 1, 1), packed)
        return packed

    def heat_rows(r, carry):
        base = pl.multiple_of(r * tall, tall)
        first = masks(tall)[1]
        fields = []
        for h in range(2):
            here = (pl.ds(base, tall), slice(128 * h, 128 * h + 128))
            tally = tally_v[here]
            sums = [None] * 4
            for l in range(nl):
                par = [jnp.concatenate([prm[l, n]] * (tall // 8), axis=0) for n in range(7)]
                t = temp_v[(l,) + here]
                heat = par[0] + (t + par[1]) / (par[2] + t * (therm_one + therm_two * t))
                heat = jnp.where(d * nl + l < tally, heat, 0.0)
                for k in range(4):
                    term = par[3 + k] * heat
                    sums[k] = term if l == 0 else sums[k] + term
            for k in range(4):
                fa[k, h, pl.ds(base + PAD, tall), :] = sums[k]
            sums.append(fa[4, h, pl.ds(base + PAD, tall), :])
            fields.append(sums)
        pack[pl.ds(base, tall), :] = pack_edges(
            [jnp.where(first, fields[0][m], fields[1][m]) for m in range(5)]
        )
        return carry

    for q in range(chunks):
        temp_copies[q].wait()
        lax.fori_loop(q * crow // tall, (q + 1) * crow // tall, heat_rows, 0)

    def send_edges(e, buf):
        for q in range(rows // 128):
            span = slice(128 * q, 128 * q + 128)
            turned = pack[span, 0:16].T
            for m in range(5):
                col_out[e, 0, m:m + 1, span] = turned[2 * m:2 * m + 1]
                col_out[e, 1, m:m + 1, span] = turned[2 * m + 1:2 * m + 2]
        for m in range(5):
            src = fa if m == 4 else buf
            for h in range(2):
                half = slice(128 * h, 128 * h + 128)
                row_out[e, 0, m:m + 1, half] = src[m, h, PAD + rows - 1:PAD + rows, :]
                row_out[e, 1, m:m + 1, half] = src[m, h, PAD:PAD + 1, :]
        to_east = pltpu.make_async_remote_copy(
            col_out.at[e, 0], col_in.at[e, 0], col_ss.at[e, 0], col_rs.at[e, 0], (d, y, east), MESH
        )
        to_west = pltpu.make_async_remote_copy(
            col_out.at[e, 1], col_in.at[e, 1], col_ss.at[e, 1], col_rs.at[e, 1], (d, y, west), MESH
        )
        to_east.start()
        to_west.start()

        @pl.when(y < last)
        def _():
            pltpu.make_async_remote_copy(
                row_out.at[e, 0], row_in.at[e, 1], row_ss.at[e, 0], row_rs.at[e, 1], (d, y + 1, b), MESH
            ).start()

        @pl.when(y == last)
        def _():
            pltpu.make_async_remote_copy(
                row_out.at[e, 0], row_in.at[e, 0], row_ss.at[e, 0], row_rs.at[e, 0], (d, y, mirror), MESH
            ).start()

        @pl.when(y > 0)
        def _():
            pltpu.make_async_remote_copy(
                row_out.at[e, 1], row_in.at[e, 0], row_ss.at[e, 1], row_rs.at[e, 0], (d, y - 1, b), MESH
            ).start()

        return to_east, to_west

    def receive_edges(e, copies):
        for copy in copies:
            copy.wait()
        north = pltpu.make_async_remote_copy(
            row_out.at[e, 0], row_in.at[e, 0], row_ss.at[e, 0], row_rs.at[e, 0], (d, y, mirror), MESH
        )
        north.wait_send()
        north.wait_recv()

        @pl.when(y > 0)
        def _():
            south = pltpu.make_async_remote_copy(
                row_out.at[e, 1], row_in.at[e, 1], row_ss.at[e, 1], row_rs.at[e, 1], (d, y - 1, b), MESH
            )
            south.wait_send()
            south.wait_recv()

        @pl.when(y == last)
        def _():
            shape = (cols, cols)
            flip = jnp.where(lanes(shape) + sublanes(shape) == cols - 1, 1.0, 0.0)
            row_in[e, 0] = jnp.dot(
                row_in[e, 0], flip, precision=lax.Precision.HIGHEST, preferred_element_type=F32
            )

        for m in range(5):
            pint[2 * m:2 * m + 1, :] = col_in[e, 1, m:m + 1, :]
            pint[2 * m + 1:2 * m + 2, :] = col_in[e, 0, m:m + 1, :]
        for q in range(rows // 128):
            span = slice(128 * q, 128 * q + 128)
            pin[span, 0:16] = pint[:, span].T

    def sweep(src, dst):
        def body(r, carry):
            base = pl.multiple_of(r * tall, tall)
            keep = [acoef[h, pl.ds(base, tall), :] for h in range(2)]
            gain = [smooth_nu * fa[4, h, pl.ds(base + PAD, tall), :] for h in range(2)]
            for k in range(4):
                here, around = neighbours(src, k, base)
                for h in range(2):
                    dst[k, h, pl.ds(base + PAD, tall), :] = keep[h] * here[h] + gain[h] * around[h]
            return carry

        lax.fori_loop(0, rows // tall, body, 0)

    def fix_rows(e, src, dst):
        for side, row in ((0, PAD + rows - 1), (1, PAD)):
            for h in range(2):
                half = slice(128 * h, 128 * h + 128)
                wet_edge = row_in[e, side, 4:5, half]
                gain = smooth_nu * fa[4, h, row:row + 1, :]
                for k in range(4):
                    more = gain * (row_in[e, side, k:k + 1, half] - wet_edge * src[k, h, row:row + 1, :])
                    dst[k, h, row:row + 1, :] = dst[k, h, row:row + 1, :] + more

    def fix_columns(src, dst, base):
        wide, first, final = masks(high)
        here = pl.ds(base + PAD, high)
        edges = pin[pl.ds(base, high), :]
        wet_edge = pltpu.roll(edges, 128 - 9, 1)
        wet = jnp.where(first, fa[4, 0, here, :], fa[4, 1, here, :])
        gain = jnp.where(jnp.logical_or(first, final), smooth_nu * wet, 0.0)
        fixed = []
        for k in range(4):
            field_edge = pltpu.roll(edges, 128 - (2 * k + 1), 1)
            old = jnp.where(first, src[k, 0, here, :], src[k, 1, here, :])
            more = gain * (field_edge - wet_edge * old)
            fixed.append(
                [
                    dst[k, 0, here, :] + jnp.where(first, more, 0.0),
                    dst[k, 1, here, :] + jnp.where(final, more, 0.0),
                ]
            )
        return fixed, wet

    edges = send_edges(0, fa)
    sweep(fa, fb)
    receive_edges(0, edges)
    fix_rows(0, fa, fb)

    def fix_first(r, carry):
        base = pl.multiple_of(r * high, high)
        first = masks(high)[1]
        fixed, wet = fix_columns(fa, fb, base)
        for k in range(4):
            for h in range(2):
                fb[k, h, pl.ds(base + PAD, high), :] = fixed[k][h]
        pack[pl.ds(base, high), :] = pack_edges(
            [jnp.where(first, fixed[k][0], fixed[k][1]) for k in range(4)] + [wet]
        )
        return carry

    lax.fori_loop(0, rows // high, fix_first, 0)
    edges = send_edges(1, fb)
    sweep(fb, fa)
    receive_edges(1, edges)
    fix_rows(1, fb, fa)

    def fix_second(r, carry):
        base = pl.multiple_of(r * high, high)
        fixed, _ = fix_columns(fb, fa, base)
        for h in range(2):
            parts = [fixed[k][h].astype(BF16).astype(F32) for k in range(4)]
            parts += [fixed[k][h] - parts[k] for k in range(4)]
            for n in range(0, high, 8):
                start = (h * rows + n) * PITCH + base * PITCH
                for m in range(8):
                    store[pl.ds(start + m, 8, stride=PITCH), :] = parts[m][n:n + 8]
        return carry

    lax.fori_loop(0, rows // high, fix_second, 0)
    small[3].wait()
    offsets.wait()

    group = lane >> 4
    v_copies = []
    for j in list(range(1, nx)) + [0]:
        c = lax.rem(b + j, nx)
        coef_copies[(j - 1) % nx].wait()

        def remap(u, carry, c=c, j=j):
            for s in range(unroll):
                g = u * unroll + s
                picked = [store[pl.ds(pick_s[c, g * 8 + p], 8), :] for p in range(8)]
                block = jnp.concatenate(picked, axis=0).astype(BF16)
                weights = coef_v[j, pl.ds(pl.multiple_of(g * 128, 128), 128), :]
                prod = lax.dot_general(
                    block, weights, (((1,), (1,)), ((), ())), preferred_element_type=F32
                )
                tight = prod[0:8]
                for p in range(1, 8):
                    tight = jnp.where(group == p, prod[p * 8:p * 8 + 8], tight)
                tight = tight[0:4] + tight[4:8]
                for k in range(4):
                    vout[lax.rem(k - d + nd, nd), j, pl.ds(g, 1), :] = tight[k:k + 1]
            return carry

        copies = []
        steps = cap // (8 * unroll)
        for part in range(parts):
            lax.fori_loop(part * steps // parts, (part + 1) * steps // parts, remap, 0)
            span = pl.ds(part * (cap // 8 // parts), cap // 8 // parts)
            for i in range(nd):
                if (i, j) != (0, 0):
                    copy = pltpu.make_async_remote_copy(
                        vout.at[i, j, span, :], vin.at[i, j, span, :],
                        v_ss.at[i, j, part], v_rs.at[i, j, part],
                        (lax.rem(d + i, nd), y, c), MESH,
                    )
                    copy.start()
                    copies.append(copy)
        v_copies.append((j, copies))

    for copy in tg_copies:
        copy.wait()
    for j in range(1, nx):
        build_onehot(j)
    gr = cap // 8
    own_group = (lanes((gr, 8, 128)) >> 4) == lax.broadcasted_iota(jnp.int32, (gr, 8, 128), 1)
    both = None
    for j, copies in v_copies:
        for copy in copies:
            copy.wait()
        summed = vout[0, 0] if j == 0 else vin[0, j]
        for i in range(1, nd):
            summed = summed + vin[i, j]
        spread = jnp.where(own_group, summed[:, None, :], 0.0).reshape(cap, 128)
        hi, lo = split_two(spread)
        eexp[j * cap:(j + 1) * cap, 0:128] = hi
        eexp[j * cap:(j + 1) * cap, 128:256] = lo
        span = slice(j * cap, (j + 1) * cap)
        part = jnp.dot(onehot[:, span], eexp[span, :], preferred_element_type=F32)
        both = part if both is None else both + part
    hi, lo = split_two(both[:, 0:128] + both[:, 128:256])
    shape = (128, 128)
    tile16 = jnp.where((lanes(shape) & 15) == (sublanes(shape) & 15), 1.0, 0.0).astype(BF16)
    spread = jnp.dot(hi, tile16, preferred_element_type=F32) + jnp.dot(
        lo, tile16, preferred_element_type=F32
    )
    result = jnp.zeros((tr, 128), F32)
    where_q = lanes((tr, 128)) >> 4
    for q in range(8):
        result = jnp.where(where_q == q, spread[q * tr:(q + 1) * tr], result)
    out_v[...] = result - base_v[...]


def per_device(sizes, temp, span, tally, sender, receiver, coef, base):
    nd, ny, nx = sizes
    nl, rows, cols = temp.shape
    cap = sender.shape[-1]
    parts = 2 if cap % 256 == 0 else 1
    unroll = min(32, cap // 8 // parts)
    blocks = rows * cols // SB
    vmem = pltpu.VMEM
    dma = pltpu.SemaphoreType.DMA
    any_spec = pl.BlockSpec(memory_space=pl.ANY)
    vspec = pl.BlockSpec(memory_space=vmem)
    tr, tc = base.shape[1:]
    scratch = [
        pltpu.SMEM((span.shape[0],), F32),
        vmem((nx, cap), jnp.int32),
        pltpu.SMEM((nx, cap), jnp.int32),
        vmem((rows, cols), jnp.int32),
        vmem((nx, cap), jnp.int32),
        vmem((nx, 1, cap), jnp.int32),
        vmem((tr, tc), F32),
        vmem((nl, rows, cols), F32),
        vmem((nx, cap * TB, SB), BF16),
        vmem((5, 2, rows + 2 * PAD, 128), F32),
        vmem((5, 2, rows + 2 * PAD, 128), F32),
        vmem((2, rows, 128), F32),
        vmem((blocks * PITCH, SB), F32),
        vmem((rows, 128), F32),
        vmem((rows, 128), F32),
        vmem((16, rows), F32),
        vmem((2, 2, 8, rows), F32),
        vmem((2, 2, 8, rows), F32),
        vmem((2, 2, 8, cols), F32),
        vmem((2, 2, 8, cols), F32),
        vmem((8, 128), F32),
        vmem((nd, 8, 128), F32),
        vmem((nl, 7, 8, 128), F32),
        vmem((nd, nx, cap // 8, 128), F32),
        vmem((nd, nx, cap // 8, 128), F32),
        vmem((nx, 1, cap), jnp.int32),
        vmem((8 * tr, nx * cap), BF16),
        vmem((nx * cap, 256), BF16),
        dma((6,)),
        dma((4,)),
        dma((nx,)),
        dma((2, 2)), dma((2, 2)),
        dma((2, 2)), dma((2, 2)),
        dma((nd,)), dma((nd,)),
        dma((nx,)), dma((nx,)),
        dma((nd, nx, parts)), dma((nd, nx, parts)),
    ]
    out = pl.pallas_call(
        functools.partial(kernel, nd, ny, nx, cap, unroll, parts),
        out_shape=pltpu.VMEM((tr, tc), F32),
        in_specs=[any_spec] * 7,
        out_specs=vspec,
        scratch_shapes=scratch,
        compiler_params=pltpu.CompilerParams(
            collective_id=0, has_side_effects=True, vmem_limit_bytes=48 * 1024 * 1024
        ),
    )(
        *[
            pltpu.with_memory_space_constraint(x, pltpu.HBM)
            for x in (
                span,
                sender.reshape(nx, cap),
                temp,
                tally,
                receiver.reshape(nx, cap),
                coef.reshape(nx, cap * TB, SB),
                base[0],
            )
        ],
    )
    return out[None]


def solution(mesh):
    sizes = tuple(mesh.shape[a] for a in ("depth", "gy", "gx"))
    return jax.shard_map(
        functools.partial(per_device, sizes),
        mesh=mesh,
        in_specs=(
            P("depth", "gy", "gx"),
            P("depth"),
            P("gy", "gx"),
            P("gy", "gx", None, None),
            P("gy", "gx", None, None),
            P("gy", "gx", None, None, None, None),
            P("depth", "gy", "gx"),
        ),
        out_specs=P("depth", "gy", "gx"),
        check_vma=False,
    )
```

```python
import functools

import jax
import jax.numpy as jnp
from jax import lax
from jax.experimental import pallas as pl
from jax.experimental.pallas import tpu as pltpu
from jax.sharding import PartitionSpec as P

SB = 128
TB = 16

cp_zero = 3991.86795711963
vol_zero = 0.00097
therm_one = 0.00017
therm_two = 5e-06
compress = 4.4e-06
bounds = (300.0, 700.0, 2000.0)
full_norm = 4000.0
smooth_nu = 0.2

MESH = pl.DeviceIdType.MESH
F32 = jnp.float32
BF16 = jnp.bfloat16
PAD = 8
PITCH = 9


def lanes(shape):
    return lax.broadcasted_iota(jnp.int32, shape, len(shape) - 1)


def sublanes(shape):
    return lax.broadcasted_iota(jnp.int32, shape, len(shape) - 2)


def split_two(x):
    hi = x.astype(BF16)
    lo = (x - hi.astype(F32)).astype(BF16)
    return hi, lo


def kernel(
    nd, ny, nx, cap, unroll, parts,
    span_h, pick_h, temp_h, tally_h, tgt_h, coef_h, base_h,
    out_v,
    span_s, pick_v, pick_s, tally_v, tgt_v, tgt_rows, base_v,
    temp_v, coef_v, fa, fb, acoef, store, pack, pin, pint,
    col_out, col_in, row_out, row_in, th_out, th_in, prm,
    vout, vin, tslot, onehot, eexp,
    in_sem, temp_sem, coef_sem, col_ss, col_rs, row_ss, row_rs, th_ss, th_rs, tg_ss, tg_rs, v_ss, v_rs,
):
    d, y, b = lax.axis_index("depth"), lax.axis_index("gy"), lax.axis_index("gx")
    nl, rows, cols = temp_v.shape
    chunks = temp_sem.shape[0]
    crow = rows // chunks
    last = ny - 1
    east, west = lax.rem(b + 1, nx), lax.rem(b + nx - 1, nx)
    mirror = nx - 1 - b

    small = []
    for n, (src, dst) in enumerate(
        ((tally_h, tally_v), (tgt_h, tgt_v), (pick_h, pick_v), (base_h, base_v), (span_h, span_s))
    ):
        copy = pltpu.make_async_copy(src, dst, in_sem.at[n])
        copy.start()
        small.append(copy)
    temp_copies = []
    for q in range(chunks):
        span = pl.ds(q * crow, crow)
        copy = pltpu.make_async_copy(temp_h.at[:, span, :], temp_v.at[:, span, :], temp_sem.at[q])
        copy.start()
        temp_copies.append(copy)
    coef_copies = []
    for j in list(range(1, nx)) + [0]:
        c = lax.rem(b + j, nx)
        copy = pltpu.make_async_copy(coef_h.at[c], coef_v.at[j], coef_sem.at[j])
        copy.start()
        coef_copies.append(copy)

    row_in[...] = jnp.zeros(row_in.shape, F32)

    barrier = pltpu.get_barrier_semaphore()
    peers = [(i, j) for i in range(nd) for j in range(nx) if (i, j) != (0, 0)]
    for i, j in peers:
        pl.semaphore_signal(
            barrier, inc=1, device_id=(lax.rem(d + i, nd), y, lax.rem(b + j, nx)), device_id_type=MESH
        )

    @pl.when(y > 0)
    def _():
        pl.semaphore_signal(barrier, inc=1, device_id=(d, y - 1, b), device_id_type=MESH)

    @pl.when(y < last)
    def _():
        pl.semaphore_signal(barrier, inc=1, device_id=(d, y + 1, b), device_id_type=MESH)

    small[4].wait()
    thick = [span_s[l] for l in range(nl)]
    total = thick[0]
    for l in range(1, nl):
        total = total + thick[l]
    th_out[...] = jnp.full(th_out.shape, total, F32)
    zero_rows = jnp.zeros((PAD, 128), F32)
    for m in range(5):
        for h in range(2):
            for buf in (fa, fb):
                buf[m, h, 0:PAD, :] = zero_rows
                buf[m, h, PAD + rows:, :] = zero_rows
    pint[...] = jnp.zeros(pint.shape, F32)
    col_out[...] = jnp.zeros(col_out.shape, F32)
    row_out[...] = jnp.zeros(row_out.shape, F32)

    lane = lanes((8, 128))
    tall, high = 64, 128

    def masks(count):
        wide = lanes((count, 128))
        return wide, wide == 0, wide == 127

    def wet_rows(r, carry):
        base = pl.multiple_of(r * high, high)
        for h in range(2):
            tally = tally_v[pl.ds(base, high), 128 * h:128 * h + 128]
            fa[4, h, pl.ds(base + PAD, high), :] = jnp.where(tally > 0, 1.0, 0.0)
        return carry

    def neighbours(buf, m, base):
        wide, first, final = masks(tall)
        here = [buf[m, h, pl.ds(base + PAD, tall), :] for h in range(2)]
        ahead = [pltpu.roll(x, 1, 1) for x in here]
        behind = [pltpu.roll(x, 127, 1) for x in here]
        left = [jnp.where(first, 0.0, ahead[0]), jnp.where(first, ahead[0], ahead[1])]
        right = [jnp.where(final, behind[1], behind[0]), jnp.where(final, 0.0, behind[1])]
        around = []
        for h in range(2):
            up = buf[m, h, pl.ds(base + PAD + 1, tall), :]
            down = buf[m, h, pl.ds(base + PAD - 1, tall), :]
            around.append((up + down) + (left[h] + right[h]))
        return here, around

    def count_rows(r, carry):
        base = pl.multiple_of(r * tall, tall)
        wet, count = neighbours(fa, 4, base)
        for h in range(2):
            acoef[h, pl.ds(base, tall), :] = 1.0 - smooth_nu * count[h]
        return carry

    tr = out_v.shape[0]

    def build_onehot(j):
        ids = tslot[j]
        for q in range(8):
            wanted = sublanes((tr, cap)) * 8 + q
            onehot[q * tr:(q + 1) * tr, j * cap:(j + 1) * cap] = jnp.where(
                wanted == ids, 1.0, 0.0
            ).astype(BF16)

    small[0].wait()
    lax.fori_loop(0, rows // high, wet_rows, 0)
    small[2].wait()
    pick_v[...] = (pick_v[...] & 1) * (rows * PITCH) + (pick_v[...] >> 1) * PITCH
    offsets = pltpu.make_async_copy(pick_v, pick_s, in_sem.at[5])
    offsets.start()
    small[1].wait()
    for j in range(nx):
        tgt_rows[j] = tgt_v[j:j + 1, :]
    tslot[0] = tgt_rows[b]

    def pack_edges(edges):
        wide = lanes(edges[0].shape)
        packed = jnp.zeros(edges[0].shape, F32)
        for m, edge in enumerate(edges):
            packed = jnp.where((wide >> 1) == m, pltpu.roll(edge, 2 * m + 1, 1), packed)
        return packed

    def raw_rows(r, carry):
        base = pl.multiple_of(r * high, high)
        first = masks(high)[1]
        here = pl.ds(base, high)
        edges = [
            jnp.where(first, temp_v[l, here, 0:128], temp_v[l, here, 128:256]) for l in range(nl)
        ]
        tally = jnp.where(first, tally_v[here, 0:128], tally_v[here, 128:256])
        pack[here, :] = pack_edges(edges + [tally.astype(F32)])
        return carry

    for copy in temp_copies:
        copy.wait()
    lax.fori_loop(0, rows // high, raw_rows, 0)

    def send_edges(e, buf):
        for q in range(rows // 128):
            span = slice(128 * q, 128 * q + 128)
            turned = pack[span, 0:16].T
            for m in range(5):
                col_out[e, 0, m:m + 1, span] = turned[2 * m:2 * m + 1]
                col_out[e, 1, m:m + 1, span] = turned[2 * m + 1:2 * m + 2]
        for m in range(5):
            src = fa if m == 4 else buf
            if buf is None:
                for side, row in ((0, rows - 1), (1, 0)):
                    line = tally_v[row:row + 1, :].astype(F32) if m == 4 else temp_v[m, row:row + 1, :]
                    row_out[e, side, m:m + 1, :] = line
                continue
            for h in range(2):
                half = slice(128 * h, 128 * h + 128)
                row_out[e, 0, m:m + 1, half] = src[m, h, PAD + rows - 1:PAD + rows, :]
                row_out[e, 1, m:m + 1, half] = src[m, h, PAD:PAD + 1, :]
        to_east = pltpu.make_async_remote_copy(
            col_out.at[e, 0], col_in.at[e, 0], col_ss.at[e, 0], col_rs.at[e, 0], (d, y, east), MESH
        )
        to_west = pltpu.make_async_remote_copy(
            col_out.at[e, 1], col_in.at[e, 1], col_ss.at[e, 1], col_rs.at[e, 1], (d, y, west), MESH
        )
        to_east.start()
        to_west.start()

        @pl.when(y < last)
        def _():
            pltpu.make_async_remote_copy(
                row_out.at[e, 0], row_in.at[e, 1], row_ss.at[e, 0], row_rs.at[e, 1], (d, y + 1, b), MESH
            ).start()

        @pl.when(y == last)
        def _():
            pltpu.make_async_remote_copy(
                row_out.at[e, 0], row_in.at[e, 0], row_ss.at[e, 0], row_rs.at[e, 0], (d, y, mirror), MESH
            ).start()

        @pl.when(y > 0)
        def _():
            pltpu.make_async_remote_copy(
                row_out.at[e, 1], row_in.at[e, 0], row_ss.at[e, 1], row_rs.at[e, 0], (d, y - 1, b), MESH
            ).start()

        return to_east, to_west

    inner = jnp.logical_and(y > 0, y < last)

    @pl.when(inner)
    def _():
        pl.semaphore_wait(barrier, len(peers) + 2)

    @pl.when(jnp.logical_not(inner))
    def _():
        pl.semaphore_wait(barrier, len(peers) + 1)

    th_copies = []
    for i in range(1, nd):
        copy = pltpu.make_async_remote_copy(
            th_out, th_in.at[i], th_ss.at[i], th_rs.at[i], (lax.rem(d + i, nd), y, b), MESH
        )
        copy.start()
        th_copies.append(copy)
    edges = send_edges(0, None)
    tg_copies = []
    for j in range(1, nx):
        c = lax.rem(b + j, nx)
        copy = pltpu.make_async_remote_copy(
            tgt_rows.at[c], tslot.at[j], tg_ss.at[j], tg_rs.at[j], (d, y, c), MESH
        )
        copy.start()
        tg_copies.append(copy)
    lax.fori_loop(0, rows // tall, count_rows, 0)
    build_onehot(0)

    top = jnp.zeros((8, 128), F32)
    for i in range(1, nd):
        th_copies[i - 1].wait()
        top = top + jnp.where(d >= i, th_in[i], 0.0)
    alpha = 10000.0 * vol_zero / cp_zero
    for l in range(nl):
        press = top + 0.5 * thick[l]
        prm[l, 0] = alpha * press
        prm[l, 1] = (0.5 * alpha * compress) * press * press
        prm[l, 2] = 1.0 - compress * press
        for k, depth in enumerate(bounds):
            prm[l, 3 + k] = jnp.clip(depth - top, 0.0, thick[l]) / depth
        prm[l, 6] = jnp.full((8, 128), thick[l] / full_norm, F32)
        top = top + thick[l]

    def heat_rows(r, carry):
        base = pl.multiple_of(r * tall, tall)
        for h in range(2):
            here = (pl.ds(base, tall), slice(128 * h, 128 * h + 128))
            tally = tally_v[here]
            sums = [None] * 4
            for l in range(nl):
                par = [jnp.concatenate([prm[l, n]] * (tall // 8), axis=0) for n in range(7)]
                t = temp_v[(l,) + here]
                heat = par[0] + (t + par[1]) / (par[2] + t * (therm_one + therm_two * t))
                heat = jnp.where(d * nl + l < tally, heat, 0.0)
                for k in range(4):
                    term = par[3 + k] * heat
                    sums[k] = term if l == 0 else sums[k] + term
            for k in range(4):
                fa[k, h, pl.ds(base + PAD, tall), :] = sums[k]
        return carry

    lax.fori_loop(0, rows // tall, heat_rows, 0)

    def edge_fields(raw):
        tally = raw[4]
        sums = [None] * 4
        for l in range(nl):
            par = [prm[l, n, 0:1, 0:1] for n in range(7)]
            t = raw[l]
            heat = par[0] + (t + par[1]) / (par[2] + t * (therm_one + therm_two * t))
            heat = jnp.where((d * nl + l).astype(F32) < tally, heat, 0.0)
            for k in range(4):
                term = par[3 + k] * heat
                sums[k] = term if l == 0 else sums[k] + term
        return sums + [jnp.where(tally > 0.0, 1.0, 0.0)]

    def receive_edges(e, copies):
        for copy in copies:
            copy.wait()
        north = pltpu.make_async_remote_copy(
            row_out.at[e, 0], row_in.at[e, 0], row_ss.at[e, 0], row_rs.at[e, 0], (d, y, mirror), MESH
        )
        north.wait_send()
        north.wait_recv()

        @pl.when(y > 0)
        def _():
            south = pltpu.make_async_remote_copy(
                row_out.at[e, 1], row_in.at[e, 1], row_ss.at[e, 1], row_rs.at[e, 1], (d, y - 1, b), MESH
            )
            south.wait_send()
            south.wait_recv()

        @pl.when(y == last)
        def _():
            shape = (cols, cols)
            flip = jnp.where(lanes(shape) + sublanes(shape) == cols - 1, 1.0, 0.0)
            row_in[e, 0] = jnp.dot(
                row_in[e, 0], flip, precision=lax.Precision.HIGHEST, preferred_element_type=F32
            )

        if e == 0:
            for side in range(2):
                fields = edge_fields([col_in[e, side, m:m + 1, :] for m in range(5)])
                for m in range(5):
                    pint[2 * m + 1 - side:2 * m + 2 - side, :] = fields[m]
                fields = edge_fields([row_in[e, side, m:m + 1, :] for m in range(5)])
                for m in range(5):
                    row_in[e, side, m:m + 1, :] = fields[m]
        else:
            for m in range(5):
                pint[2 * m:2 * m + 1, :] = col_in[e, 1, m:m + 1, :]
                pint[2 * m + 1:2 * m + 2, :] = col_in[e, 0, m:m + 1, :]
        for q in range(rows // 128):
            span = slice(128 * q, 128 * q + 128)
            pin[span, 0:16] = pint[:, span].T

    def sweep(src, dst):
        def body(r, carry):
            base = pl.multiple_of(r * tall, tall)
            keep = [acoef[h, pl.ds(base, tall), :] for h in range(2)]
            gain = [smooth_nu * fa[4, h, pl.ds(base + PAD, tall), :] for h in range(2)]
            for k in range(4):
                here, around = neighbours(src, k, base)
                for h in range(2):
                    dst[k, h, pl.ds(base + PAD, tall), :] = keep[h] * here[h] + gain[h] * around[h]
            return carry

        lax.fori_loop(0, rows // tall, body, 0)

    def fix_rows(e, src, dst):
        for side, row in ((0, PAD + rows - 1), (1, PAD)):
            for h in range(2):
                half = slice(128 * h, 128 * h + 128)
                wet_edge = row_in[e, side, 4:5, half]
                gain = smooth_nu * fa[4, h, row:row + 1, :]
                for k in range(4):
                    more = gain * (row_in[e, side, k:k + 1, half] - wet_edge * src[k, h, row:row + 1, :])
                    dst[k, h, row:row + 1, :] = dst[k, h, row:row + 1, :] + more

    def fix_columns(src, dst, base):
        wide, first, final = masks(high)
        here = pl.ds(base + PAD, high)
        edges = pin[pl.ds(base, high), :]
        wet_edge = pltpu.roll(edges, 128 - 9, 1)
        wet = jnp.where(first, fa[4, 0, here, :], fa[4, 1, here, :])
        gain = jnp.where(jnp.logical_or(first, final), smooth_nu * wet, 0.0)
        fixed = []
        for k in range(4):
            field_edge = pltpu.roll(edges, 128 - (2 * k + 1), 1)
            old = jnp.where(first, src[k, 0, here, :], src[k, 1, here, :])
            more = gain * (field_edge - wet_edge * old)
            fixed.append(
                [
                    dst[k, 0, here, :] + jnp.where(first, more, 0.0),
                    dst[k, 1, here, :] + jnp.where(final, more, 0.0),
                ]
            )
        return fixed, wet

    sweep(fa, fb)
    receive_edges(0, edges)
    fix_rows(0, fa, fb)

    def fix_first(r, carry):
        base = pl.multiple_of(r * high, high)
        first = masks(high)[1]
        fixed, wet = fix_columns(fa, fb, base)
        for k in range(4):
            for h in range(2):
                fb[k, h, pl.ds(base + PAD, high), :] = fixed[k][h]
        pack[pl.ds(base, high), :] = pack_edges(
            [jnp.where(first, fixed[k][0], fixed[k][1]) for k in range(4)] + [wet]
        )
        return carry

    lax.fori_loop(0, rows // high, fix_first, 0)
    edges = send_edges(1, fb)
    sweep(fb, fa)
    receive_edges(1, edges)
    fix_rows(1, fb, fa)

    def fix_second(r, carry):
        base = pl.multiple_of(r * high, high)
        fixed, _ = fix_columns(fb, fa, base)
        for h in range(2):
            parts = [fixed[k][h].astype(BF16).astype(F32) for k in range(4)]
            parts += [fixed[k][h] - parts[k] for k in range(4)]
            for n in range(0, high, 8):
                start = (h * rows + n) * PITCH + base * PITCH
                for m in range(8):
                    store[pl.ds(start + m, 8, stride=PITCH), :] = parts[m][n:n + 8]
        return carry

    lax.fori_loop(0, rows // high, fix_second, 0)
    small[3].wait()
    offsets.wait()

    group = lane >> 4
    v_copies = []
    for j in list(range(1, nx)) + [0]:
        c = lax.rem(b + j, nx)
        coef_copies[(j - 1) % nx].wait()

        def remap(u, carry, c=c, j=j):
            for s in range(unroll):
                g = u * unroll + s
                picked = [store[pl.ds(pick_s[c, g * 8 + p], 8), :] for p in range(8)]
                block = jnp.concatenate(picked, axis=0).astype(BF16)
                weights = coef_v[j, pl.ds(pl.multiple_of(g * 128, 128), 128), :]
                prod = lax.dot_general(
                    block, weights, (((1,), (1,)), ((), ())), preferred_element_type=F32
                )
                tight = prod[0:8]
                for p in range(1, 8):
                    tight = jnp.where(group == p, prod[p * 8:p * 8 + 8], tight)
                tight = tight[0:4] + tight[4:8]
                for k in range(4):
                    vout[lax.rem(k - d + nd, nd), j, pl.ds(g, 1), :] = tight[k:k + 1]
            return carry

        copies = []
        steps = cap // (8 * unroll)
        for part in range(parts):
            lax.fori_loop(part * steps // parts, (part + 1) * steps // parts, remap, 0)
            span = pl.ds(part * (cap // 8 // parts), cap // 8 // parts)
            for i in range(nd):
                if (i, j) != (0, 0):
                    copy = pltpu.make_async_remote_copy(
                        vout.at[i, j, span, :], vin.at[i, j, span, :],
                        v_ss.at[i, j, part], v_rs.at[i, j, part],
                        (lax.rem(d + i, nd), y, c), MESH,
                    )
                    copy.start()
                    copies.append(copy)
        v_copies.append((j, copies))

    for copy in tg_copies:
        copy.wait()
    for j in range(1, nx):
        build_onehot(j)
    gr = cap // 8
    own_group = (lanes((gr, 8, 128)) >> 4) == lax.broadcasted_iota(jnp.int32, (gr, 8, 128), 1)
    both = None
    for j, copies in v_copies:
        for copy in copies:
            copy.wait()
        summed = vout[0, 0] if j == 0 else vin[0, j]
        for i in range(1, nd):
            summed = summed + vin[i, j]
        spread = jnp.where(own_group, summed[:, None, :], 0.0).reshape(cap, 128)
        hi, lo = split_two(spread)
        eexp[j * cap:(j + 1) * cap, 0:128] = hi
        eexp[j * cap:(j + 1) * cap, 128:256] = lo
        span = slice(j * cap, (j + 1) * cap)
        part = jnp.dot(onehot[:, span], eexp[span, :], preferred_element_type=F32)
        both = part if both is None else both + part
    hi, lo = split_two(both[:, 0:128] + both[:, 128:256])
    shape = (128, 128)
    tile16 = jnp.where((lanes(shape) & 15) == (sublanes(shape) & 15), 1.0, 0.0).astype(BF16)
    spread = jnp.dot(hi, tile16, preferred_element_type=F32) + jnp.dot(
        lo, tile16, preferred_element_type=F32
    )
    result = jnp.zeros((tr, 128), F32)
    where_q = lanes((tr, 128)) >> 4
    for q in range(8):
        result = jnp.where(where_q == q, spread[q * tr:(q + 1) * tr], result)
    out_v[...] = result - base_v[...]


def per_device(sizes, temp, span, tally, sender, receiver, coef, base):
    nd, ny, nx = sizes
    nl, rows, cols = temp.shape
    cap = sender.shape[-1]
    parts = 2 if cap % 256 == 0 else 1
    unroll = min(32, cap // 8 // parts)
    blocks = rows * cols // SB
    vmem = pltpu.VMEM
    dma = pltpu.SemaphoreType.DMA
    any_spec = pl.BlockSpec(memory_space=pl.ANY)
    vspec = pl.BlockSpec(memory_space=vmem)
    tr, tc = base.shape[1:]
    scratch = [
        pltpu.SMEM((span.shape[0],), F32),
        vmem((nx, cap), jnp.int32),
        pltpu.SMEM((nx, cap), jnp.int32),
        vmem((rows, cols), jnp.int32),
        vmem((nx, cap), jnp.int32),
        vmem((nx, 1, cap), jnp.int32),
        vmem((tr, tc), F32),
        vmem((nl, rows, cols), F32),
        vmem((nx, cap * TB, SB), BF16),
        vmem((5, 2, rows + 2 * PAD, 128), F32),
        vmem((5, 2, rows + 2 * PAD, 128), F32),
        vmem((2, rows, 128), F32),
        vmem((blocks * PITCH, SB), F32),
        vmem((rows, 128), F32),
        vmem((rows, 128), F32),
        vmem((16, rows), F32),
        vmem((2, 2, 8, rows), F32),
        vmem((2, 2, 8, rows), F32),
        vmem((2, 2, 8, cols), F32),
        vmem((2, 2, 8, cols), F32),
        vmem((8, 128), F32),
        vmem((nd, 8, 128), F32),
        vmem((nl, 7, 8, 128), F32),
        vmem((nd, nx, cap // 8, 128), F32),
        vmem((nd, nx, cap // 8, 128), F32),
        vmem((nx, 1, cap), jnp.int32),
        vmem((8 * tr, nx * cap), BF16),
        vmem((nx * cap, 256), BF16),
        dma((6,)),
        dma((4,)),
        dma((nx,)),
        dma((2, 2)), dma((2, 2)),
        dma((2, 2)), dma((2, 2)),
        dma((nd,)), dma((nd,)),
        dma((nx,)), dma((nx,)),
        dma((nd, nx, parts)), dma((nd, nx, parts)),
    ]
    out = pl.pallas_call(
        functools.partial(kernel, nd, ny, nx, cap, unroll, parts),
        out_shape=pltpu.VMEM((tr, tc), F32),
        in_specs=[any_spec] * 7,
        out_specs=vspec,
        scratch_shapes=scratch,
        compiler_params=pltpu.CompilerParams(
            collective_id=0, has_side_effects=True, vmem_limit_bytes=48 * 1024 * 1024
        ),
    )(
        *[
            pltpu.with_memory_space_constraint(x, pltpu.HBM)
            for x in (
                span,
                sender.reshape(nx, cap),
                temp,
                tally,
                receiver.reshape(nx, cap),
                coef.reshape(nx, cap * TB, SB),
                base[0],
            )
        ],
    )
    return out[None]


def solution(mesh):
    sizes = tuple(mesh.shape[a] for a in ("depth", "gy", "gx"))
    return jax.shard_map(
        functools.partial(per_device, sizes),
        mesh=mesh,
        in_specs=(
            P("depth", "gy", "gx"),
            P("depth"),
            P("gy", "gx"),
            P("gy", "gx", None, None),
            P("gy", "gx", None, None),
            P("gy", "gx", None, None, None, None),
            P("depth", "gy", "gx"),
        ),
        out_specs=P("depth", "gy", "gx"),
        check_vma=False,
    )
```
